128 devices in a mesh: aux: 16 (over y, x), orb: 8 (over z, core).
Axes of the slice: x: 4, y: 4, z: 4, core: 2. Of those that a mesh axis runs over, the one named last changes fastest.
Arguments:
- integrals: bfloat16 [256, 64, 16384], P(('aux', 'orb')), may hold values from -0.75 to 0.75
- tile_mu: int32 [256], P(('aux', 'orb')), may hold values from 0 to 31
- tile_nu: int32 [256], P(('aux', 'orb')), may hold values from 0 to 31
- live_count: int32 [128], P(('aux', 'orb')), may hold values from 1 to 2, as said below
- support: int32 [64, 16], replicated, may hold values from 0 to 31, as said below
- coeffs: bfloat16 [64, 1024], replicated, may hold values from -0.75 to 0.75
- pair_mu: int32 [512], replicated, may hold values from 0 to 31, as said below
- pair_nu: int32 [512], replicated, may hold values from 0 to 31
Outputs:
- exchange: float32 [512, 4096], P(('aux', 'orb'))
The draws below stay inside these ranges and needn't reach their ends.
Inputs may be any that keep to these rules, and one draw needn't show every extreme that they name: A device's live integral slots are its first live_count ones; some device has all 2 live. An orbital's 16 support tiles are distinct. The pairs (pair_mu, pair_nu) are distinct and pair_mu != pair_nu.
All inputs are finite; a program needn't handle non-finite values.
Results may differ from the reference program's by a relative error of at most 0.004.
Values may be sent and summed in bfloat16 or wider, within the bound.
A program may use at most 128 MiB of HBM per device.

```python
import jax
import jax.numpy as jnp
from jax import lax

TILE = 64
AUX_DEV = 256
OCC = 64
SUP = 16
WT = 32
NT_DEV = 2
AUX = 4096
TILES = 256
NPAIR = 512
N_AUX = 16
N_ORB = 8


def draw_live_count(key, part):
    devices_all = N_AUX * N_ORB
    counts = jax.random.randint(jax.random.fold_in(key, 11), (devices_all,), max(1, NT_DEV // 4), NT_DEV + 1)
    fullest = jax.random.randint(jax.random.fold_in(key, 12), (), 0, devices_all)
    return jnp.where(jnp.arange(devices_all) == fullest, NT_DEV, counts).astype(jnp.int32)


def draw_support(key, part):
    centre = jax.random.randint(jax.random.fold_in(key, 21), (OCC, 1), 0, WT)
    return ((centre + jnp.arange(SUP, dtype=jnp.int32)[None, :]) % WT).astype(jnp.int32)


def pair_table(key):
    chosen = jax.random.permutation(jax.random.fold_in(key, 31), WT * (WT - 1))[:NPAIR]
    row_tile = chosen // (WT - 1)
    rest = chosen % (WT - 1)
    col_tile = rest + (rest >= row_tile).astype(jnp.int32)
    return (row_tile.astype(jnp.int32), col_tile.astype(jnp.int32))


def draw_pair_mu(key, part):
    return pair_table(key)[0]


def draw_pair_nu(key, part):
    return pair_table(key)[1]


def plant(entries, own_key, least, top_value):
    place = [jax.random.randint(jax.random.fold_in(own_key, axis), (), 0, length) for axis, length in enumerate(entries.shape)]
    longest = entries.shape.index(max(entries.shape))
    beside = place[:longest] + [(place[longest] + 1) % entries.shape[longest]] + place[longest + 1:]
    return entries.at[tuple(place)].set(least).at[tuple(beside)].set(top_value)


def level_of(key, extent, split, smallest, top_value):
    gain, own = 1.0, jax.random.fold_in(key, 6)
    for axis_at, parts in split:
        draws = jnp.exp(jax.random.uniform(jax.random.fold_in(own, axis_at), (parts,), jnp.float32, smallest / len(split), top_value / len(split)))
        gain = gain * jnp.repeat(draws, extent[axis_at] // parts).reshape([-1 if axis == axis_at else 1 for axis in range(len(extent))])
    return gain


def scatter_about(key, dims, deviation, most, shards=(), kind=jnp.bfloat16):
    result = deviation * jax.random.normal(key, dims, jnp.float32)
    if shards:
        result = result * level_of(key, dims, shards, -0.22, 0.18)
    return jnp.clip(result, -most, most).astype(kind)


def setup_inputs(seed: int = 0) -> dict:
    arg_keys = jax.random.split(jax.random.key(seed), 9)
    integrals = scatter_about(arg_keys[0], (TILES, TILE, AUX_DEV * TILE), (1.0 / (AUX * OCC * SUP // WT) ** 0.25), 0.75, ((0, 128),))
    tile_mu = plant(jax.random.randint(arg_keys[1], (TILES,), 0, WT), jax.random.fold_in(arg_keys[1], 1), 0, WT - 1).astype(jnp.int32)
    tile_nu = plant(jax.random.randint(arg_keys[2], (TILES,), 0, WT), jax.random.fold_in(arg_keys[2], 1), 0, WT - 1).astype(jnp.int32)
    live_count = draw_live_count(jax.random.fold_in(arg_keys[8], 71), 0)
    support = draw_support(jax.random.fold_in(arg_keys[8], 71), 0)
    coeffs = scatter_about(arg_keys[5], (OCC, SUP * TILE), TILE ** -0.5, 0.75)
    pair_mu = draw_pair_mu(jax.random.fold_in(arg_keys[8], 71), 0)
    pair_nu = draw_pair_nu(jax.random.fold_in(arg_keys[8], 71), 0)
    return dict(integrals=integrals, tile_mu=tile_mu, tile_nu=tile_nu, live_count=live_count, support=support, coeffs=coeffs, pair_mu=pair_mu, pair_nu=pair_nu)


def coefficients(support, coeffs):
    onehot = (support[:, :, None] == jnp.arange(WT, dtype=jnp.int32)[None, None, :]).astype(jnp.float32)
    blocks = coeffs.reshape(OCC, SUP, TILE).astype(jnp.float32)
    table = jnp.einsum("osw,osn->wno", onehot, blocks, precision=lax.Precision.HIGHEST)
    return table.astype(jnp.bfloat16)


def reference(integrals, tile_mu, tile_nu, live_count, support, coeffs, pair_mu, pair_nu):
    coeff_table = coefficients(support, coeffs)
    slab_slots = N_ORB * NT_DEV
    slab_ints = integrals.reshape(N_AUX, slab_slots, TILE, AUX_DEV * TILE)
    slab_mu = tile_mu.reshape(N_AUX, slab_slots)
    slab_nu = tile_nu.reshape(N_AUX, slab_slots)
    slots = jnp.arange(NT_DEV, dtype=jnp.int32)
    live_rows = (slots[None, :] < live_count[:, None]).astype(jnp.float32).reshape(N_AUX, slab_slots)

    def one_slab(packed):
        ints_a, mu_a, nu_a, live_a = packed
        picked = coeff_table[nu_a].astype(jnp.float32)
        products = jnp.einsum("kni,knx->kix", picked, ints_a.astype(jnp.float32), precision=lax.Precision.HIGHEST)
        products = products * live_a[:, None, None]
        onehot = (jnp.arange(WT, dtype=jnp.int32)[:, None] == mu_a[None, :]).astype(jnp.float32)
        summed = jnp.dot(onehot, products.reshape(slab_slots, OCC * AUX_DEV * TILE), precision=lax.Precision.HIGHEST)
        summed = summed.reshape(WT, OCC, AUX_DEV, TILE).transpose(0, 3, 1, 2)
        return summed.astype(jnp.bfloat16)

    stacked = lax.map(one_slab, (slab_ints, slab_mu, slab_nu, live_rows))
    halves = jnp.moveaxis(stacked, 0, 2).reshape(WT, TILE, N_AUX * OCC * AUX_DEV)

    def one_pair(pair):
        left_tiles = lax.dynamic_index_in_dim(halves, pair[0], 0, keepdims=False)
        right_tiles = lax.dynamic_index_in_dim(halves, pair[1], 0, keepdims=False)
        tile_block = jnp.dot(left_tiles, right_tiles.T, preferred_element_type=jnp.float32)
        return tile_block.reshape(TILE * TILE)

    pairs = jnp.stack([pair_mu, pair_nu], axis=1).astype(jnp.int32)
    return lax.map(one_pair, pairs)
```

```python
import functools

import jax
import jax.numpy as jnp
from jax import lax
from jax.experimental import pallas as pl
from jax.experimental.pallas import tpu as pltpu
from jax.sharding import PartitionSpec as P

TILE = 64
AUX_DEV = 256
OCC = 64
SUP = 16
WT = 32
N_ORB = 8
SLOTS = 16
QS = 4
COLS = AUX_DEV * TILE // (QS * N_ORB)
ROWS = COLS // 128 * OCC
MESH = pl.DeviceIdType.MESH
VMEM = pl.BlockSpec(memory_space=pltpu.VMEM)
SMEM = pl.BlockSpec(memory_space=pltpu.SMEM)
LIMIT = 60 * 1024 * 1024

OFFSETS = ((2, 0), (2, 1), (1, 0), (3, 0), (1, 1), (3, 1), (0, 1))


def gram_kernel(
    nu_ref,
    live_ref,
    support_ref,
    coeffs_ref,
    mu_ref,
    ints_hbm,
    g_ref,
    mus_ref,
    ints,
    sbuf,
    rbuf,
    gsend,
    gpeer,
    in_sem,
    send_sem,
    recv_sem,
    mu_send,
    mu_recv,
    g_send,
    g_recv,
):
    aux = lax.axis_index("aux")
    me = lax.axis_index("orb")
    z, core = me // 2, lax.rem(me, 2)
    others = [lax.rem(z + dz, 4) * 2 + lax.rem(core + dc, 2) for dz, dc in OFFSETS]
    peer = others[-1]

    loads = []
    for q in range(QS):
        load = pltpu.make_async_copy(
            ints_hbm.at[:, :, pl.ds(q * COLS * N_ORB, COLS * N_ORB)], ints.at[q], in_sem.at[q]
        )
        load.start()
        loads.append(load)

    barrier = pltpu.get_barrier_semaphore()
    for other in others:
        pl.semaphore_signal(barrier, inc=1, device_id=(aux, other), device_id_type=MESH)

    lane = lax.broadcasted_iota(jnp.int32, (OCC, 128), 1)
    low = lane < TILE
    support = support_ref[...]
    halves = []
    for s in range(2):
        acc = jnp.zeros((OCC, 128), jnp.float32)
        for jj in range(SUP // 2):
            tile = jnp.where(low, support[:, 2 * jj : 2 * jj + 1], support[:, 2 * jj + 1 : 2 * jj + 2])
            block = coeffs_ref[:, jj * 128 : (jj + 1) * 128].astype(jnp.float32)
            acc = acc + jnp.where(tile == nu_ref[s], block, 0.0)
        acc = acc + pltpu.roll(acc, 64, 1)
        live = jnp.where(s < live_ref[0], 1.0, 0.0)
        keep = low if s == 0 else jnp.logical_not(low)
        halves.append(jnp.where(keep, acc * live, 0.0))
    coef = jnp.concatenate(halves, axis=0).astype(jnp.bfloat16)

    pl.semaphore_wait(barrier, len(others))
    mu_copies = []
    for t, other in enumerate(others):
        copy = pltpu.make_async_remote_copy(
            src_ref=mu_ref,
            dst_ref=mus_ref.at[me],
            send_sem=mu_send.at[t],
            recv_sem=mu_recv.at[me],
            device_id=(aux, other),
            device_id_type=MESH,
        )
        copy.start()
        mu_copies.append(copy)
    mus_ref[me] = mu_ref[...]

    def products(q, dest, store):
        block = ints[q, :, :, pl.ds(pl.multiple_of(dest * COLS, COLS), COLS)].reshape(2 * TILE, COLS)
        res = jnp.dot(coef, block, preferred_element_type=jnp.float32)
        for p in range(COLS // 128):
            a = res[:OCC, p * 128 : (p + 1) * 128]
            b = res[OCC:, p * 128 : (p + 1) * 128]
            even = jnp.where(low, a, pltpu.roll(b, 64, 1))
            odd = jnp.where(low, pltpu.roll(a, 64, 1), b)
            store(p * OCC, even.astype(jnp.bfloat16))
            store(ROWS + p * OCC, odd.astype(jnp.bfloat16))

    def data_copy(q, t):
        return pltpu.make_async_remote_copy(
            src_ref=sbuf.at[q, t],
            dst_ref=rbuf.at[q, me],
            send_sem=send_sem.at[q, t],
            recv_sem=recv_sem.at[q, me],
            device_id=(aux, others[t]),
            device_id_type=MESH,
        )

    for q in range(QS):
        loads[q].wait()
    g_ref[...] = jnp.zeros_like(g_ref)

    @pl.loop(0, QS)
    def _(q):
        for t, other in enumerate(others):

            def to_send(row, value):
                sbuf[q, t, row : row + OCC, :] = value

            products(q, other, to_send)
            data_copy(q, t).start()

        def to_own(row, value):
            rbuf[q, me, row : row + OCC, :] = value

        products(q, me, to_own)

    @pl.loop(0, QS)
    def _(q):
        for other in others:
            pltpu.make_async_remote_copy(
                src_ref=sbuf.at[q, 0],
                dst_ref=rbuf.at[q, other],
                send_sem=send_sem.at[q, 0],
                recv_sem=recv_sem.at[q, other],
                device_id=(aux, other),
                device_id_type=MESH,
            ).wait_recv()

        @pl.loop(0, 4)
        def _(r):
            left = jnp.concatenate([rbuf[q, 2 * r], rbuf[q, 2 * r + 1]], axis=1)
            for c in range(4):
                right = jnp.concatenate([rbuf[q, 2 * c], rbuf[q, 2 * c + 1]], axis=1)
                g_ref[pl.ds(pl.multiple_of(r * 256, 256), 256), c * 256 : (c + 1) * 256] += lax.dot_general(
                    left, right, (((0,), (0,)), ((), ())), preferred_element_type=jnp.float32
                )

    gsend[...] = g_ref[...].astype(jnp.bfloat16)
    swap = pltpu.make_async_remote_copy(
        src_ref=gsend,
        dst_ref=gpeer,
        send_sem=g_send,
        recv_sem=g_recv,
        device_id=(aux, peer),
        device_id_type=MESH,
    )
    swap.start()
    for t, other in enumerate(others):
        mu_copies[t].wait_send()
        pltpu.make_async_remote_copy(
            src_ref=mu_ref,
            dst_ref=mus_ref.at[other],
            send_sem=mu_send.at[t],
            recv_sem=mu_recv.at[other],
            device_id=(aux, other),
            device_id_type=MESH,
        ).wait_recv()

    @pl.loop(0, QS)
    def _(q):
        for t in range(len(others)):
            data_copy(q, t).wait_send()

    swap.wait()
    g_ref[...] += gpeer[...].astype(jnp.float32)


def slab_gram(nu, live, support, coeffs, mu, ints):
    dma = pltpu.SemaphoreType.DMA
    return pl.pallas_call(
        gram_kernel,
        out_shape=(
            jax.ShapeDtypeStruct((SLOTS * TILE, SLOTS * TILE), jnp.float32),
            jax.ShapeDtypeStruct((N_ORB, 8, 128), jnp.int32),
        ),
        in_specs=[SMEM, SMEM, VMEM, VMEM, VMEM, pl.BlockSpec(memory_space=pl.ANY)],
        out_specs=(VMEM, VMEM),
        scratch_shapes=[
            pltpu.VMEM((QS, 2, TILE, COLS * N_ORB), jnp.bfloat16),
            pltpu.VMEM((QS, N_ORB - 1, 2 * ROWS, 128), jnp.bfloat16),
            pltpu.VMEM((QS, N_ORB, 2 * ROWS, 128), jnp.bfloat16),
            pltpu.VMEM((SLOTS * TILE, SLOTS * TILE), jnp.bfloat16),
            pltpu.VMEM((SLOTS * TILE, SLOTS * TILE), jnp.bfloat16),
            dma((QS,)),
            dma((QS, N_ORB - 1)),
            dma((QS, N_ORB)),
            dma((N_ORB - 1,)),
            dma((N_ORB,)),
            dma(()),
            dma(()),
        ],
        compiler_params=pltpu.CompilerParams(
            collective_id=0, has_side_effects=True, vmem_limit_bytes=LIMIT
        ),
        name="slab_gram",
    )(nu, live, support, coeffs, mu, ints)


def pick_kernel(mu_ref, pm_ref, pn_ref, g_in, a_ref, b_ref, g, first):
    core = lax.rem(lax.axis_index("orb"), 2)
    lane = lax.broadcasted_iota(jnp.int32, (TILE, 128), 1)
    low = lane < TILE

    @pl.loop(0, WT)
    def _(w):
        first[w] = SLOTS

    for s in reversed(range(SLOTS)):
        first[mu_ref[s]] = s
    g[...] = g_in[...]

    @pl.loop(1, SLOTS)
    def _(t):
        u = first[mu_ref[t]]

        @pl.when(u < t)
        def _():
            to = pl.ds(pl.multiple_of(u * TILE, TILE), TILE)
            g[to, :] += g[pl.ds(pl.multiple_of(t * TILE, TILE), TILE), :]

    @pl.loop(1, SLOTS)
    def _(t):
        u = first[mu_ref[t]]

        @pl.when(u < t)
        def _():
            shift = lax.rem(t + u, 2) * TILE
            keep = (lane >= TILE) == (lax.rem(u, 2) == 1)

            @pl.loop(0, SLOTS)
            def _(r):
                rows = pl.ds(pl.multiple_of(r * TILE, TILE), TILE)
                source = g[rows, pl.ds(pl.multiple_of(t // 2 * 128, 128), 128)]
                to = pl.ds(pl.multiple_of(u // 2 * 128, 128), 128)
                g[rows, to] += jnp.where(keep, pltpu.roll(source, shift, 1), 0.0)

    def tile_of(k, half):
        u, v = first[pm_ref[k]], first[pn_ref[k]]
        there = jnp.logical_and(u < SLOTS, v < SLOTS)
        u, v = jnp.minimum(u, SLOTS - 1), jnp.minimum(v, SLOTS - 1)
        rows = pl.ds(pl.multiple_of(u * TILE, TILE), TILE)
        tile = g[rows, pl.ds(pl.multiple_of(v // 2 * 128, 128), 128)]
        shift = lax.rem(v + half, 2) * TILE
        return pltpu.roll(tile, shift, 1) * jnp.where(there, 1.0, 0.0)

    @pl.loop(0, 64)
    def _(b):
        y, x, zz = b // 16, lax.rem(b // 4, 4), lax.rem(b, 4)
        k = b // 4 * 32 + zz * 8 + core * 4
        a_ref[x, y, zz] = jnp.where(low, tile_of(k, 0), tile_of(k + 1, 1)).astype(jnp.bfloat16)
        b_ref[y, x, zz] = jnp.where(low, tile_of(k + 2, 0), tile_of(k + 3, 1)).astype(jnp.bfloat16)


def pick(mus, pair_mu, pair_nu, gram):
    half = jax.ShapeDtypeStruct((4, 4, 4, TILE, 128), jnp.bfloat16)
    return pl.pallas_call(
        pick_kernel,
        out_shape=(half, half),
        in_specs=[SMEM, SMEM, SMEM, VMEM],
        out_specs=(VMEM, VMEM),
        scratch_shapes=[
            pltpu.VMEM((SLOTS * TILE, SLOTS * TILE), jnp.float32),
            pltpu.SMEM((WT,), jnp.int32),
        ],
        compiler_params=pltpu.CompilerParams(vmem_limit_bytes=LIMIT),
        name="pick",
    )(mus, pair_mu, pair_nu, gram)


def reduce_kernel(
    a_ref, b_ref, out_ref, ra1, rb1, sa, sb, ra2, rb2, sz, rz, send_sem, recv_sem
):
    aux, orb = lax.axis_index("aux"), lax.axis_index("orb")
    y, x, z, core = aux // 4, lax.rem(aux, 4), orb // 2, lax.rem(orb, 2)

    def along(axis, step):
        if axis == "x":
            return (y * 4 + lax.rem(x + step, 4), orb)
        if axis == "y":
            return (lax.rem(y + step, 4) * 4 + x, orb)
        return (aux, lax.rem(z + step, 4) * 2 + core)

    place = {"x": x, "y": y, "z": z}
    barrier = pltpu.get_barrier_semaphore()
    for axis in "xyz":
        for step in (1, 2, 3):
            pl.semaphore_signal(barrier, inc=1, device_id=along(axis, step), device_id_type=MESH)
    pl.semaphore_wait(barrier, 9)

    def send(stage, axis, source, landing):
        copies = []
        here = place[axis]
        for step in (2, 1, 3):
            there = lax.rem(here + step, 4)
            copy = pltpu.make_async_remote_copy(
                src_ref=source.at[there],
                dst_ref=landing.at[4 - step - 1],
                send_sem=send_sem.at[stage, step - 1],
                recv_sem=recv_sem.at[stage, 4 - step - 1],
                device_id=along(axis, step),
                device_id_type=MESH,
            )
            copy.start()
            copies.append(copy)
        return copies

    def total(axis, source, landing, rest):
        own = source[(place[axis],) + rest].astype(jnp.float32)
        for i in range(3):
            own = own + landing[(i,) + rest].astype(jnp.float32)
        return own

    copies_a = send(0, "x", a_ref, ra1)
    copies_b = send(1, "y", b_ref, rb1)
    for copy in copies_a:
        copy.wait_recv()
    for i in range(4):
        sa[i] = total("x", a_ref, ra1, (i,)).astype(jnp.bfloat16)
    more_a = send(2, "y", sa, ra2)
    for copy in copies_b:
        copy.wait_recv()
    for i in range(4):
        sb[i] = total("y", b_ref, rb1, (i,)).astype(jnp.bfloat16)
    more_b = send(3, "x", sb, rb2)
    for copy in more_a:
        copy.wait_recv()
    for i in range(4):
        sz[i, 0] = total("y", sa, ra2, (i,)).astype(jnp.bfloat16)
    for copy in more_b:
        copy.wait_recv()
    for i in range(4):
        sz[i, 1] = total("x", sb, rb2, (i,)).astype(jnp.bfloat16)
    last = send(4, "z", sz, rz)
    for copy in last:
        copy.wait_recv()
    out_ref[...] = total("z", sz, rz, ())
    for copy in copies_a + copies_b + more_a + more_b + last:
        copy.wait_send()


def reduce_pairs(a, b):
    dma = pltpu.SemaphoreType.DMA
    bf16 = jnp.bfloat16
    return pl.pallas_call(
        reduce_kernel,
        out_shape=jax.ShapeDtypeStruct((2, TILE, 128), jnp.float32),
        in_specs=[VMEM, VMEM],
        out_specs=VMEM,
        scratch_shapes=[
            pltpu.VMEM((3, 4, 4, TILE, 128), bf16),
            pltpu.VMEM((3, 4, 4, TILE, 128), bf16),
            pltpu.VMEM((4, 4, TILE, 128), bf16),
            pltpu.VMEM((4, 4, TILE, 128), bf16),
            pltpu.VMEM((3, 4, TILE, 128), bf16),
            pltpu.VMEM((3, 4, TILE, 128), bf16),
            pltpu.VMEM((4, 2, TILE, 128), bf16),
            pltpu.VMEM((3, 2, TILE, 128), bf16),
            dma((5, 3)),
            dma((5, 3)),
        ],
        compiler_params=pltpu.CompilerParams(
            collective_id=1, has_side_effects=True, vmem_limit_bytes=LIMIT
        ),
        name="reduce_pairs",
    )(a, b)


def on_device(integrals, tile_mu, tile_nu, live_count, support, coeffs, pair_mu, pair_nu):
    mu = jnp.broadcast_to(tile_mu[:, None], (2, 128))
    mu = jnp.concatenate([mu] * 4, axis=0)
    gram, mus = slab_gram(tile_nu, live_count, support, coeffs, mu, integrals)
    mus = mus[:, :2, 0].reshape(SLOTS)
    a, b = pick(mus, pair_mu, pair_nu, gram)
    out = reduce_pairs(a, b)
    return out.reshape(2, TILE, 2, TILE).transpose(0, 2, 1, 3).reshape(4, TILE * TILE)


def solution(mesh):
    return jax.shard_map(
        on_device,
        mesh=mesh,
        in_specs=(
            P(("aux", "orb"), None, None),
            P(("aux", "orb")),
            P(("aux", "orb")),
            P(("aux", "orb")),
            P(),
            P(),
            P(),
            P(),
        ),
        out_specs=P(("aux", "orb"), None),
        check_vma=False,
    )
```

```python
import functools

import jax
import jax.numpy as jnp
from jax import lax
from jax.experimental import pallas as pl
from jax.experimental.pallas import tpu as pltpu
from jax.sharding import PartitionSpec as P

TILE = 64
AUX_DEV = 256
OCC = 64
SUP = 16
WT = 32
N_ORB = 8
POOL = 96
SLOTS = 16
QS = 4
COLS = AUX_DEV * TILE // (QS * N_ORB)
ROWS = COLS // 128 * OCC
MESH = pl.DeviceIdType.MESH
VMEM = pl.BlockSpec(memory_space=pltpu.VMEM)
SMEM = pl.BlockSpec(memory_space=pltpu.SMEM)
LIMIT = 60 * 1024 * 1024

OFFSETS = ((2, 0), (2, 1), (1, 0), (3, 0), (1, 1), (3, 1), (0, 1))


def gram_kernel(
    pool,
    mu_ref,
    nu_ref,
    live_ref,
    support_ref,
    coeffs_ref,
    pm_ref,
    pn_ref,
    ints_hbm,
    g_ref,
    where_ref,
    over_ref,
    ints,
    sbuf,
    rbuf,
    xbuf,
    tiles,
    unpack,
    acc,
    gsend,
    gpeer,
    mine,
    mus,
    in_sem,
    send_sem,
    recv_sem,
    mu_send,
    mu_recv,
    g_send,
    g_recv,
):
    aux = lax.axis_index("aux")
    me = lax.axis_index("orb")
    z, core = me // 2, lax.rem(me, 2)
    others = [lax.rem(z + dz, 4) * 2 + lax.rem(core + dc, 2) for dz, dc in OFFSETS]
    peer = others[-1]

    def load(q):
        return pltpu.make_async_copy(
            ints_hbm.at[:, :, pl.ds(pl.multiple_of(q * COLS * N_ORB, COLS * N_ORB), COLS * N_ORB)],
            ints.at[q],
            in_sem.at[q],
        )

    barrier = pltpu.get_barrier_semaphore()
    for other in others:
        pl.semaphore_signal(barrier, inc=1, device_id=(aux, other), device_id_type=MESH)
    for q in range(QS):
        load(q).start()

    lane = lax.broadcasted_iota(jnp.int32, (OCC, 128), 1)
    low = lane < TILE
    one = (
        lax.broadcasted_iota(jnp.int32, (SUP, SUP), 0) == lax.broadcasted_iota(jnp.int32, (SUP, SUP), 1)
    ).astype(jnp.float32)
    support = lax.dot_general(
        support_ref[...].astype(jnp.float32), one, (((0,), (0,)), ((), ())), preferred_element_type=jnp.float32
    )
    halves = []
    for s in range(2):
        total = jnp.zeros((OCC, 128), jnp.float32)
        nu = nu_ref[s].astype(jnp.float32)
        for jj in range(SUP // 2):
            tile = jnp.where(low, support[:, 2 * jj : 2 * jj + 1], support[:, 2 * jj + 1 : 2 * jj + 2])
            block = coeffs_ref[:, jj * 128 : (jj + 1) * 128].astype(jnp.float32)
            total = total + jnp.where(tile == nu, block, 0.0)
        total = total + pltpu.roll(total, 64, 1)
        live = jnp.where(s < live_ref[0], 1.0, 0.0)
        keep = low if s == 0 else jnp.logical_not(low)
        halves.append(jnp.where(keep, total * live, 0.0))
    coef = jnp.concatenate(halves, axis=0).astype(jnp.bfloat16)

    slot = lax.rem(lax.broadcasted_iota(jnp.int32, (8, 128), 0), 2)
    mine[0] = jnp.where(slot < live_ref[0], jnp.where(slot == 0, mu_ref[0], mu_ref[1]), -1)
    mine[1] = jnp.where(slot < live_ref[0], jnp.where(slot == 0, nu_ref[0], nu_ref[1]), -1)

    for j in range(SUP):
        tiles[j] = jnp.broadcast_to(support[:, j : j + 1], (OCC, 128))
    square = (2 * OCC, 2 * OCC)
    to, at = lax.broadcasted_iota(jnp.int32, square, 0), lax.broadcasted_iota(jnp.int32, square, 1)
    before = jnp.where(at < to, 1.0, 0.0).astype(jnp.bfloat16)

    def placement(nus):
        used = []
        for s in range(2):
            nu = nus[s : s + 1].astype(jnp.float32)
            count = jnp.zeros((OCC, 128), jnp.float32)
            for j in range(SUP):
                count = count + jnp.where(tiles[j] == nu, 1.0, 0.0)
            used.append(count)
        used = jnp.concatenate(used, axis=0)
        rank = jnp.dot(before, used.astype(jnp.bfloat16), preferred_element_type=jnp.float32)
        last = slice(2 * OCC - 1, 2 * OCC)
        placed = jnp.where(rank == at.astype(jnp.float32), used, 0.0)
        return placed.astype(jnp.bfloat16), rank[last] + used[last]

    own, _ = placement(mine[1])
    packed = lax.dot_general(own, coef, (((0,), (0,)), ((), ())), preferred_element_type=jnp.float32)
    packed = packed[:pool].astype(jnp.bfloat16)

    def mu_copy(t, device):
        return pltpu.make_async_remote_copy(
            src_ref=mine,
            dst_ref=mus.at[device],
            send_sem=mu_send.at[t],
            recv_sem=mu_recv.at[device],
            device_id=(aux, others[t]),
            device_id_type=MESH,
        )

    def data_copy(q, t, device):
        return pltpu.make_async_remote_copy(
            src_ref=sbuf.at[q, t],
            dst_ref=rbuf.at[q, device],
            send_sem=send_sem.at[q, t],
            recv_sem=recv_sem.at[q, device],
            device_id=(aux, others[t]),
            device_id_type=MESH,
        )

    def swap(r):
        rows = pl.ds(r * 256, 256)
        return pltpu.make_async_remote_copy(
            src_ref=gsend.at[rows],
            dst_ref=gpeer.at[rows],
            send_sem=g_send.at[r],
            recv_sem=g_recv.at[r],
            device_id=(aux, peer),
            device_id_type=MESH,
        )

    def products(q, dest, store):
        block = ints[q, :, :, pl.ds(pl.multiple_of(dest * COLS, COLS), COLS)].reshape(2 * TILE, COLS)
        res = jnp.dot(packed, block, preferred_element_type=jnp.float32).astype(jnp.bfloat16)
        for p in range(COLS // 128):
            store(p * pool, res[:, p * 128 : (p + 1) * 128])

    pl.semaphore_wait(barrier, len(others))
    for t in range(len(others)):
        mu_copy(t, me).start()

    @pl.loop(0, QS)
    def _(q):
        load(q).wait()
        for t, other in enumerate(others):

            def to_send(row, value):
                sbuf[q, t, row : row + pool, :] = value

            products(q, other, to_send)
            data_copy(q, t, me).start()

        def to_own(row, value):
            rbuf[q, me, row : row + pool, :] = value

        products(q, me, to_own)

    mus[me] = mine[...]
    for t, other in enumerate(others):
        mu_copy(t, other).wait_recv()
    over_ref[...] = jnp.zeros_like(over_ref)

    @pl.loop(0, N_ORB)
    def _(source):
        placed, rows = placement(mus[source, 1])
        unpack[source] = placed
        over_ref[...] = jnp.maximum(over_ref[...], jnp.where(rows > pool, 1.0, 0.0))

    table = mus[:, 0].reshape(N_ORB * 8, 128)[:, :1]
    count = pm_ref.shape[1]
    k = lax.broadcasted_iota(jnp.int32, (N_ORB * 8, count), 1)
    here = lax.rem(k // 4, 2) == core
    rows = jnp.where(table == pm_ref[...], 1.0, 0.0).astype(jnp.bfloat16)
    cols = jnp.logical_and(table == pn_ref[...], here)

    def pairs(value):
        return lax.dot_general(
            rows,
            jnp.where(cols, value.astype(jnp.float32), 0.0).astype(jnp.bfloat16),
            (((1,), (1,)), ((), ())),
            preferred_element_type=jnp.float32,
        )

    found = pairs(k // 32) * 32.0 + pairs(lax.rem(k, 32) + 1) - 1.0
    where_ref[...] = found.astype(jnp.int32)

    acc[...] = jnp.zeros_like(acc)

    def spread(q, source):
        data = rbuf[q, source]
        data = jnp.concatenate([data[p * pool : (p + 1) * pool] for p in range(COLS // 128)], axis=1)
        res = jnp.dot(unpack[source][:, :pool], data, preferred_element_type=jnp.float32)
        for p in range(COLS // 128):
            a = res[:OCC, p * 128 : (p + 1) * 128]
            b = res[OCC:, p * 128 : (p + 1) * 128]
            even = jnp.where(low, a, pltpu.roll(b, 64, 1))
            odd = jnp.where(low, pltpu.roll(a, 64, 1), b)
            xbuf[source, p * OCC : (p + 1) * OCC] = even.astype(jnp.bfloat16)
            xbuf[source, ROWS + p * OCC : ROWS + (p + 1) * OCC] = odd.astype(jnp.bfloat16)

    def gram(r):
        left = jnp.concatenate([xbuf[2 * r], xbuf[2 * r + 1]], axis=1)
        for c in range(4):
            right = jnp.concatenate([xbuf[2 * c], xbuf[2 * c + 1]], axis=1)
            acc[r, :, c * 256 : (c + 1) * 256] += lax.dot_general(
                left, right, (((0,), (0,)), ((), ())), preferred_element_type=jnp.float32
            )

    @pl.loop(0, QS)
    def _(q):
        spread(q, me)
        for t in reversed(range(len(others))):
            data_copy(q, t, others[t]).wait_recv()
            spread(q, others[t])

        @pl.when(q < QS - 1)
        def _():
            @pl.loop(0, 4)
            def _(r):
                gram(r)

    for r in range(4):
        gram(r)
        gsend[r * 256 : (r + 1) * 256] = acc[r].astype(jnp.bfloat16)
        swap(r).start()
    for r in range(4):
        swap(r).wait_recv()
        rows = slice(r * 256, (r + 1) * 256)
        g_ref[rows] = (acc[r] + gpeer[rows].astype(jnp.float32)).astype(jnp.bfloat16)

    for r in range(4):
        swap(r).wait_send()
    for t in range(len(others)):
        mu_copy(t, me).wait_send()

    @pl.loop(0, QS)
    def _(q):
        for t in range(len(others)):
            data_copy(q, t, me).wait_send()


def slab_gram(pool, identity, mu, nu, live, support, coeffs, pair_mu, pair_nu, ints):
    dma = pltpu.SemaphoreType.DMA
    size = SLOTS * TILE
    return pl.pallas_call(
        functools.partial(gram_kernel, pool),
        out_shape=(
            jax.ShapeDtypeStruct((size, size), jnp.bfloat16),
            jax.ShapeDtypeStruct((N_ORB * 8, N_ORB * 8), jnp.int32),
            jax.ShapeDtypeStruct((8, 128), jnp.float32),
        ),
        in_specs=[SMEM] * 3 + [VMEM] * 4 + [pl.BlockSpec(memory_space=pl.ANY)],
        out_specs=(VMEM, VMEM, VMEM),
        scratch_shapes=[
            pltpu.VMEM((QS, 2, TILE, COLS * N_ORB), jnp.bfloat16),
            pltpu.VMEM((QS, N_ORB - 1, COLS // 128 * pool, 128), jnp.bfloat16),
            pltpu.VMEM((QS, N_ORB, COLS // 128 * pool, 128), jnp.bfloat16),
            pltpu.VMEM((N_ORB, 2 * ROWS, 128), jnp.bfloat16),
            pltpu.VMEM((SUP, OCC, 128), jnp.float32),
            pltpu.VMEM((N_ORB, 2 * OCC, 2 * OCC), jnp.bfloat16),
            pltpu.VMEM((4, size // 4, size), jnp.float32),
            pltpu.VMEM((size, size), jnp.bfloat16),
            pltpu.VMEM((size, size), jnp.bfloat16),
            pltpu.VMEM((2, 8, 128), jnp.int32),
            pltpu.VMEM((N_ORB, 2, 8, 128), jnp.int32),
            dma((QS,)),
            dma((QS, N_ORB - 1)),
            dma((QS, N_ORB)),
            dma((N_ORB - 1,)),
            dma((N_ORB,)),
            dma((4,)),
            dma((4,)),
        ],
        compiler_params=pltpu.CompilerParams(
            collective_id=identity, has_side_effects=True, vmem_limit_bytes=LIMIT
        ),
        name="slab_gram",
    )(mu, nu, live, support, coeffs, pair_mu, pair_nu, ints)


def pick_kernel(where_ref, g_ref, e_ref):
    lane = lax.broadcasted_iota(jnp.int32, (TILE, 128), 1)
    high = jnp.where(lane < TILE, 0, 1)
    e_ref[...] = jnp.zeros_like(e_ref)

    @pl.loop(0, SLOTS)
    def _(s):
        rows = pl.ds(pl.multiple_of(s * TILE, TILE), TILE)
        for t in range(SLOTS):
            k = where_ref[s // 2 * 8 + lax.rem(s, 2), t // 2 * 8 + t % 2]

            @pl.when(k >= 0)
            def _():
                half, pair, zz = lax.rem(k, 2), lax.rem(k // 2, 2), lax.rem(k // 8, 4)
                x, y = lax.rem(k // 32, 4), k // 128
                slow, fast = jnp.where(pair == 0, x, y), jnp.where(pair == 0, y, x)
                tile = g_ref[rows, t // 2 * 128 : (t // 2 + 1) * 128].astype(jnp.float32)
                tile = jnp.where(half == t % 2, tile, pltpu.roll(tile, 64, 1))
                e_ref[pair, slow, fast, zz] += jnp.where(high == half, tile, 0.0).astype(jnp.bfloat16)


def pick(where, gram):
    return pl.pallas_call(
        pick_kernel,
        out_shape=jax.ShapeDtypeStruct((2, 4, 4, 4, TILE, 128), jnp.bfloat16),
        in_specs=[SMEM, VMEM],
        out_specs=VMEM,
        compiler_params=pltpu.CompilerParams(vmem_limit_bytes=LIMIT),
        name="pick",
    )(where, gram)


def reduce_kernel(
    e_ref, over_ref, out_ref, any_ref, ra1, rb1, sa, sb, ra2, rb2, sz, rz, done, row, overs, send_sem, recv_sem
):
    aux, orb = lax.axis_index("aux"), lax.axis_index("orb")
    y, x, z, core = aux // 4, lax.rem(aux, 4), orb // 2, lax.rem(orb, 2)

    def along(axis, step):
        if axis == "x":
            return (y * 4 + lax.rem(x + step, 4), orb)
        if axis == "y":
            return (lax.rem(y + step, 4) * 4 + x, orb)
        return (aux, lax.rem(z + step, 4) * 2 + core)

    place = {"x": x, "y": y, "z": z}
    barrier = pltpu.get_barrier_semaphore()
    for axis in "xyz":
        for step in (1, 2, 3):
            pl.semaphore_signal(barrier, inc=1, device_id=along(axis, step), device_id_type=MESH)
    pl.semaphore_wait(barrier, 9)

    def send(stage, axis, source, landing):
        copies = []
        here = place[axis]
        for step in (2, 1, 3):
            there = lax.rem(here + step, 4)
            copy = pltpu.make_async_remote_copy(
                src_ref=source.at[there],
                dst_ref=landing.at[4 - step - 1],
                send_sem=send_sem.at[stage, step - 1],
                recv_sem=recv_sem.at[stage, 4 - step - 1],
                device_id=along(axis, step),
                device_id_type=MESH,
            )
            copy.start()
            copies.append(copy)
        return copies

    def total(axis, source, landing, rest):
        own = source[(place[axis],) + rest].astype(jnp.float32)
        for i in range(3):
            own = own + landing[(i,) + rest].astype(jnp.float32)
        return own

    def tell(stage, axis, source):
        copies = []
        for step in (1, 2, 3):
            copy = pltpu.make_async_remote_copy(
                src_ref=source,
                dst_ref=overs.at[stage - 5, 4 - step - 1],
                send_sem=send_sem.at[stage, step - 1],
                recv_sem=recv_sem.at[stage, 4 - step - 1],
                device_id=along(axis, step),
                device_id_type=MESH,
            )
            copy.start()
            copies.append(copy)
        return copies

    a_ref, b_ref = e_ref.at[0], e_ref.at[1]
    tell_x = tell(5, "x", over_ref)
    copies_a = send(0, "x", a_ref, ra1)
    copies_b = send(1, "y", b_ref, rb1)
    for copy in copies_a:
        copy.wait_recv()
    for copy in tell_x:
        copy.wait_recv()
    row[...] = over_ref[...] + overs[0, 0] + overs[0, 1] + overs[0, 2]
    tell_y = tell(6, "y", row)
    for i in range(4):
        sa[i] = total("x", a_ref, ra1, (i,)).astype(jnp.bfloat16)
    more_a = send(2, "y", sa, ra2)
    for copy in copies_b:
        copy.wait_recv()
    for i in range(4):
        sb[i] = total("y", b_ref, rb1, (i,)).astype(jnp.bfloat16)
    more_b = send(3, "x", sb, rb2)
    for copy in more_a:
        copy.wait_recv()
    for i in range(4):
        sz[i, 0] = total("y", sa, ra2, (i,))
    for copy in more_b:
        copy.wait_recv()
    for i in range(4):
        sz[i, 1] = total("x", sb, rb2, (i,))
    last = send(4, "z", sz, rz)
    for copy in last:
        copy.wait_recv()
    lane = lax.broadcasted_iota(jnp.int32, (TILE // 2, 128), 1)
    low = lane < TILE
    for copy in tell_y:
        copy.wait_recv()
    found = jnp.max(row[...] + overs[1, 0] + overs[1, 1] + overs[1, 2])
    any_ref[0] = jnp.where(found > 0.5, 1, 0)
    done[...] = total("z", sz, rz, ())
    for i in range(2):
        even = done[i, pl.ds(0, TILE // 2, stride=2), :]
        odd = done[i, pl.ds(1, TILE // 2, stride=2), :]
        first = jnp.where(low, even, pltpu.roll(odd, 64, 1))
        second = jnp.where(low, pltpu.roll(even, 64, 1), odd)
        for m in range(TILE // 2):
            out_ref[2 * i : 2 * i + 1, m * 128 : (m + 1) * 128] = first[m : m + 1]
            out_ref[2 * i + 1 : 2 * i + 2, m * 128 : (m + 1) * 128] = second[m : m + 1]
    for copy in copies_a + copies_b + more_a + more_b + last + tell_x + tell_y:
        copy.wait_send()


def reduce_pairs(identity, e, over):
    dma = pltpu.SemaphoreType.DMA
    bf16 = jnp.bfloat16
    return pl.pallas_call(
        reduce_kernel,
        out_shape=(
            jax.ShapeDtypeStruct((4, TILE * TILE), jnp.float32),
            jax.ShapeDtypeStruct((1,), jnp.int32),
        ),
        in_specs=[VMEM, VMEM],
        out_specs=(VMEM, SMEM),
        scratch_shapes=[
            pltpu.VMEM((3, 4, 4, TILE, 128), bf16),
            pltpu.VMEM((3, 4, 4, TILE, 128), bf16),
            pltpu.VMEM((4, 4, TILE, 128), bf16),
            pltpu.VMEM((4, 4, TILE, 128), bf16),
            pltpu.VMEM((3, 4, TILE, 128), bf16),
            pltpu.VMEM((3, 4, TILE, 128), bf16),
            pltpu.VMEM((4, 2, TILE, 128), jnp.float32),
            pltpu.VMEM((3, 2, TILE, 128), jnp.float32),
            pltpu.VMEM((2, TILE, 128), jnp.float32),
            pltpu.VMEM((8, 128), jnp.float32),
            pltpu.VMEM((2, 3, 8, 128), jnp.float32),
            dma((7, 3)),
            dma((7, 3)),
        ],
        compiler_params=pltpu.CompilerParams(
            collective_id=identity, has_side_effects=True, vmem_limit_bytes=LIMIT
        ),
        name="reduce_pairs",
    )(e, over)


def on_device(integrals, tile_mu, tile_nu, live_count, support, coeffs, pair_mu, pair_nu):
    args = (tile_mu, tile_nu, live_count, support.T, coeffs, pair_mu[None, :], pair_nu[None, :], integrals)

    def exchange(pool, identity):
        gram, where, over = slab_gram(pool, identity, *args)
        return reduce_pairs(identity + 1, pick(where, gram), over)

    out, over = exchange(POOL, 0)
    return lax.cond(over[0] == 0, lambda: out, lambda: exchange(2 * OCC, 2)[0])


def solution(mesh):
    return jax.shard_map(
        on_device,
        mesh=mesh,
        in_specs=(
            P(("aux", "orb"), None, None),
            P(("aux", "orb")),
            P(("aux", "orb")),
            P(("aux", "orb")),
            P(),
            P(),
            P(),
            P(),
        ),
        out_specs=P(("aux", "orb"), None),
        check_vma=False,
    )
```

```python
import functools

import jax
import jax.numpy as jnp
from jax import lax
from jax.experimental import pallas as pl
from jax.experimental.pallas import tpu as pltpu
from jax.sharding import PartitionSpec as P

TILE = 64
AUX_DEV = 256
OCC = 64
SUP = 16
WT = 32
N_ORB = 8
POOL = 96
SLOTS = 16
QS = 4
COLS = AUX_DEV * TILE // (QS * N_ORB)
ROWS = COLS // 128 * OCC
CUT = 48
MESH = pl.DeviceIdType.MESH
VMEM = pl.BlockSpec(memory_space=pltpu.VMEM)
SMEM = pl.BlockSpec(memory_space=pltpu.SMEM)
LIMIT = 60 * 1024 * 1024

OFFSETS = ((2, 0), (2, 1), (1, 0), (3, 0), (1, 1), (3, 1), (0, 1))


STEPS = (2, 1, 3)
BLOCKS = 17 * 16


def exchange_kernel(
    pool,
    mu_ref,
    nu_ref,
    live_ref,
    support_ref,
    coeffs_ref,
    pm_ref,
    pn_ref,
    ints_hbm,
    out_ref,
    any_ref,
    ints,
    sbuf,
    rbuf,
    xbuf,
    tiles,
    unpack,
    merge,
    stack,
    first,
    acc,
    gsend,
    gpeer,
    blocks,
    index,
    index_smem,
    mine,
    mus,
    over,
    row,
    overs,
    done,
    e_a,
    e_b,
    e_c,
    r1_a,
    r1_b,
    r1_c,
    s2_a,
    s2_b,
    s2_c,
    r2_a,
    r2_b,
    r2_c,
    s3_a,
    s3_b,
    s3_c,
    r3_a,
    r3_b,
    r3_c,
    in_sem,
    send_sem,
    recv_sem,
    mu_send,
    mu_recv,
    g_send,
    g_recv,
    index_sem,
    tell_send,
    tell_recv,
    ring_send,
    ring_recv,
):
    aux = lax.axis_index("aux")
    me = lax.axis_index("orb")
    y, x = aux // 4, lax.rem(aux, 4)
    z, core = me // 2, lax.rem(me, 2)
    others = [lax.rem(z + dz, 4) * 2 + lax.rem(core + dc, 2) for dz, dc in OFFSETS]
    peer = others[-1]
    place = {"x": x, "y": y, "z": z}

    def along(axis, step):
        if axis == "x":
            return (y * 4 + lax.rem(x + step, 4), me)
        if axis == "y":
            return (lax.rem(y + step, 4) * 4 + x, me)
        return (aux, lax.rem(z + step, 4) * 2 + core)

    def load(q):
        return pltpu.make_async_copy(
            ints_hbm.at[:, :, pl.ds(pl.multiple_of(q * COLS * N_ORB, COLS * N_ORB), COLS * N_ORB)],
            ints.at[q],
            in_sem.at[q],
        )

    barrier = pltpu.get_barrier_semaphore()
    for other in others:
        pl.semaphore_signal(barrier, inc=1, device_id=(aux, other), device_id_type=MESH)
    for axis in "xy":
        for step in STEPS:
            pl.semaphore_signal(barrier, inc=1, device_id=along(axis, step), device_id_type=MESH)
    for q in range(QS):
        load(q).start()

    lane = lax.broadcasted_iota(jnp.int32, (OCC, 128), 1)
    low = lane < TILE
    one = (
        lax.broadcasted_iota(jnp.int32, (SUP, SUP), 0) == lax.broadcasted_iota(jnp.int32, (SUP, SUP), 1)
    ).astype(jnp.float32)
    support = lax.dot_general(
        support_ref[...].astype(jnp.float32), one, (((0,), (0,)), ((), ())), preferred_element_type=jnp.float32
    )
    halves = []
    for s in range(2):
        total = jnp.zeros((OCC, 128), jnp.float32)
        nu = nu_ref[s].astype(jnp.float32)
        for jj in range(SUP // 2):
            tile = jnp.where(low, support[:, 2 * jj : 2 * jj + 1], support[:, 2 * jj + 1 : 2 * jj + 2])
            block = coeffs_ref[:, jj * 128 : (jj + 1) * 128].astype(jnp.float32)
            total = total + jnp.where(tile == nu, block, 0.0)
        total = total + pltpu.roll(total, 64, 1)
        live = jnp.where(s < live_ref[0], 1.0, 0.0)
        keep = low if s == 0 else jnp.logical_not(low)
        halves.append(jnp.where(keep, total * live, 0.0))
    coef = jnp.concatenate(halves, axis=0).astype(jnp.bfloat16)

    slot = lax.rem(lax.broadcasted_iota(jnp.int32, (8, 128), 0), 2)
    mine[0] = jnp.where(slot < live_ref[0], jnp.where(slot == 0, mu_ref[0], mu_ref[1]), -1)
    mine[1] = jnp.where(slot < live_ref[0], jnp.where(slot == 0, nu_ref[0], nu_ref[1]), -1)

    for j in range(SUP):
        tiles[j] = jnp.broadcast_to(support[:, j : j + 1], (OCC, 128))
    square = (2 * OCC, 2 * OCC)
    to, at = lax.broadcasted_iota(jnp.int32, square, 0), lax.broadcasted_iota(jnp.int32, square, 1)
    before = jnp.where(at < to, 1.0, 0.0).astype(jnp.bfloat16)

    def placement(nus):
        used = []
        for s in range(2):
            nu = nus[s : s + 1].astype(jnp.float32)
            count = jnp.zeros((OCC, 128), jnp.float32)
            for j in range(SUP):
                count = count + jnp.where(tiles[j] == nu, 1.0, 0.0)
            used.append(count)
        used = jnp.concatenate(used, axis=0)
        rank = jnp.dot(before, used.astype(jnp.bfloat16), preferred_element_type=jnp.float32)
        last = slice(2 * OCC - 1, 2 * OCC)
        placed = jnp.where(rank == at.astype(jnp.float32), used, 0.0)
        return placed.astype(jnp.bfloat16), rank[last] + used[last]

    own, _ = placement(mine[1])
    packed = lax.dot_general(own, coef, (((0,), (0,)), ((), ())), preferred_element_type=jnp.float32)
    packed = packed[:pool].astype(jnp.bfloat16)

    def mu_copy(t, device):
        return pltpu.make_async_remote_copy(
            src_ref=mine,
            dst_ref=mus.at[device],
            send_sem=mu_send.at[t],
            recv_sem=mu_recv.at[device],
            device_id=(aux, others[t]),
            device_id_type=MESH,
        )

    def data_copy(q, t, device):
        return pltpu.make_async_remote_copy(
            src_ref=sbuf.at[q, t],
            dst_ref=rbuf.at[q, device],
            send_sem=send_sem.at[q, t],
            recv_sem=recv_sem.at[q, device],
            device_id=(aux, others[t]),
            device_id_type=MESH,
        )

    def swap(r):
        rows = pl.ds(r * 256, 256)
        return pltpu.make_async_remote_copy(
            src_ref=gsend.at[rows],
            dst_ref=gpeer.at[rows],
            send_sem=g_send.at[r],
            recv_sem=g_recv.at[r],
            device_id=(aux, peer),
            device_id_type=MESH,
        )

    def products(q, dest, store):
        block = ints[q, :, :, pl.ds(pl.multiple_of(dest * COLS, COLS), COLS)].reshape(2 * TILE, COLS)
        res = jnp.dot(packed, block, preferred_element_type=jnp.float32).astype(jnp.bfloat16)
        for p in range(COLS // 128):
            store(p * pool, res[:, p * 128 : (p + 1) * 128])

    def tell(stage, axis, source):
        return [
            pltpu.make_async_remote_copy(
                src_ref=source,
                dst_ref=overs.at[stage, 3 - step],
                send_sem=tell_send.at[stage, step - 1],
                recv_sem=tell_recv.at[stage, 3 - step],
                device_id=along(axis, step),
                device_id_type=MESH,
            )
            for step in STEPS
        ]

    pl.semaphore_wait(barrier, len(others) + 6)
    for t in range(len(others)):
        mu_copy(t, me).start()

    @pl.loop(0, QS)
    def _(q):
        load(q).wait()
        for t, other in enumerate(others):

            def to_send(row, value):
                sbuf[q, t, row : row + pool, :] = value

            products(q, other, to_send)
            data_copy(q, t, me).start()

        def to_own(row, value):
            rbuf[q, me, row : row + pool, :] = value

        products(q, me, to_own)

    mus[me] = mine[...]
    for t, other in enumerate(others):
        mu_copy(t, other).wait_recv()
    over[...] = jnp.zeros_like(over)

    @pl.loop(0, N_ORB)
    def _(source):
        placed, rows = placement(mus[source, 1])
        unpack[source] = placed.astype(jnp.float32).T
        over[...] = jnp.maximum(over[...], jnp.where(rows > pool, 1.0, 0.0))

    tell_x = tell(0, "x", over)
    for copy in tell_x:
        copy.start()

    def mu_of(slot):
        return mus[slot // 2, 0, slot % 2 : slot % 2 + 1]

    for s in range(SLOTS):
        is_first = jnp.ones((1, 128), jnp.int32)
        for t in range(s):
            is_first = jnp.where(mu_of(t) == mu_of(s), 0, is_first)
        first[s : s + 1] = jnp.where(mu_of(s) >= 0, is_first, 0)
    low_row = low[:1]
    for pair in range(N_ORB):

        @pl.loop(0, N_ORB)
        def _(source):
            def shares(slot, s):
                same = mus[source, 0, s : s + 1] == mu_of(slot)
                return jnp.where(same, first[slot : slot + 1], 0).astype(jnp.float32)

            kept = jnp.where(low_row, shares(2 * pair, 0), shares(2 * pair + 1, 1))
            turned = jnp.where(low_row, shares(2 * pair, 1), shares(2 * pair + 1, 0))
            placed = unpack[source]
            both = placed * kept + pltpu.roll(placed, 64, 1) * turned
            at_row = pl.ds(pl.multiple_of(source * pool, pool), pool)
            stack[at_row] = both[:pool]

        merge[pair] = stack[...].T.astype(jnp.bfloat16)

    k = lax.broadcasted_iota(jnp.int32, pm_ref.shape, 1)
    u = jnp.full(pm_ref.shape, SLOTS, jnp.int32)
    v = jnp.full(pm_ref.shape, -1, jnp.int32)
    for s in range(SLOTS):
        known = first[s : s + 1, :1] > 0
        tile = mu_of(s)[:, :1]
        u = jnp.where(jnp.logical_and(known, pm_ref[...] == tile), s, u)
        v = jnp.where(jnp.logical_and(known, pn_ref[...] == tile), s, v)
    u = jnp.where(v >= 0, u, SLOTS)
    v = jnp.maximum(v, 0)
    index[...] = (((v + k) & 1) * 8 + (v >> 1)) * 17 + u
    to_smem = pltpu.make_async_copy(index, index_smem, index_sem)
    to_smem.start()
    for c in range(16):
        blocks[c * 17 + 16] = jnp.zeros((TILE, 128), jnp.bfloat16)

    for copy in tell_x:
        copy.wait_recv()
    row[...] = over[...] + overs[0, 0] + overs[0, 1] + overs[0, 2]
    tell_y = tell(1, "y", row)
    for copy in tell_y:
        copy.start()

    acc[...] = jnp.zeros_like(acc)

    def spread(q):
        @pl.loop(0, N_ORB)
        def _(pair):
            data = jnp.concatenate(
                [
                    jnp.concatenate([rbuf[q, source, p * pool : (p + 1) * pool] for source in range(N_ORB)], axis=0)
                    for p in range(COLS // 128)
                ],
                axis=1,
            )
            res = jnp.dot(merge[pair], data, preferred_element_type=jnp.float32)
            for p in range(COLS // 128):
                a = res[:OCC, p * 128 : (p + 1) * 128]
                b = res[OCC:, p * 128 : (p + 1) * 128]
                even = jnp.where(low, a, pltpu.roll(b, 64, 1))
                odd = jnp.where(low, pltpu.roll(a, 64, 1), b)
                xbuf[pair, p * OCC : (p + 1) * OCC] = even.astype(jnp.bfloat16)
                xbuf[pair, ROWS + p * OCC : ROWS + (p + 1) * OCC] = odd.astype(jnp.bfloat16)

    def gram(r):
        left = jnp.concatenate([xbuf[2 * r], xbuf[2 * r + 1]], axis=1)
        for c in range(4):
            right = jnp.concatenate([xbuf[2 * c], xbuf[2 * c + 1]], axis=1)
            acc[r, :, c * 256 : (c + 1) * 256] += lax.dot_general(
                left, right, (((0,), (0,)), ((), ())), preferred_element_type=jnp.float32
            )

    @pl.loop(0, QS)
    def _(q):
        for t, other in enumerate(others):
            data_copy(q, t, other).wait_recv()
        spread(q)

        @pl.when(q < QS - 1)
        def _():
            @pl.loop(0, 4)
            def _(r):
                gram(r)

    for r in range(4):
        gram(r)
        gsend[r * 256 : (r + 1) * 256] = acc[r].astype(jnp.bfloat16)
        swap(r).start()
    for r in range(4):
        swap(r).wait_recv()
        for c in range(8):
            lanes = slice(c * 128, (c + 1) * 128)
            total = acc[r, :, lanes] + gpeer[r * 256 : (r + 1) * 256, lanes].astype(jnp.float32)
            turned = pltpu.roll(total, 64, 1)
            for i in range(4):
                rows = slice(i * TILE, (i + 1) * TILE)
                blocks[c * 17 + r * 4 + i] = total[rows].astype(jnp.bfloat16)
                blocks[(8 + c) * 17 + r * 4 + i] = turned[rows].astype(jnp.bfloat16)

    to_smem.wait()

    def block(yy, xx, zz, j):
        k = (yy * 4 + xx) * 32 + zz * 8 + core * 4 + 2 * j
        return jnp.where(low, blocks[index_smem[0, k]], blocks[index_smem[0, k + 1]])

    axes = ("xyz", "yzx", "zxy")

    def ring(part, stage, source, landing, steps=STEPS):
        axis = axes[part][stage]
        at = part * 3 + stage
        return [
            pltpu.make_async_remote_copy(
                src_ref=source.at[lax.rem(place[axis] + step, 4)],
                dst_ref=landing.at[3 - step],
                send_sem=ring_send.at[at, step - 1],
                recv_sem=ring_recv.at[at, 3 - step],
                device_id=along(axis, step),
                device_id_type=MESH,
            )
            for step in steps
        ]

    def begin(copies):
        for copy in copies:
            copy.start()
        return copies

    def arrive(copies):
        for copy in copies:
            copy.wait_recv()

    everything = []
    one = [[], [], []]
    for step in STEPS + (0,):
        xx = lax.rem(x + step, 4)

        @pl.loop(0, 16)
        def _(i):
            yy, zz = i // 4, lax.rem(i, 4)
            value = block(yy, xx, zz, 0)
            e_a[xx, yy, zz] = value[:CUT]
            e_c[zz, xx, yy, 0] = value[CUT:]

        if step:
            one[0] += begin(ring(0, 0, e_a, r1_a, (step,)))
        yy = lax.rem(y + step, 4)

        @pl.loop(0, 16)
        def _(i):
            zz, xx = i // 4, lax.rem(i, 4)
            value = block(yy, xx, zz, 1)
            e_b[yy, zz, xx] = value[:CUT]
            e_c[zz, xx, yy, 1] = value[CUT:]

        if step:
            one[1] += begin(ring(1, 0, e_b, r1_b, (step,)))
    one[2] = begin(ring(2, 0, e_c, r1_c))

    def total(part, stage, source, landing, i):
        at = place[axes[part][stage]]
        value = source[at, i].astype(jnp.float32)
        for n in range(3):
            value = value + landing[n, i].astype(jnp.float32)
        return value

    two, three = [], []
    for part, (e, r1, s2, r2) in enumerate(((e_a, r1_a, s2_a, r2_a), (e_b, r1_b, s2_b, r2_b), (e_c, r1_c, s2_c, r2_c))):
        arrive(one[part])
        for i in range(4):
            s2[i] = total(part, 0, e, r1, i).astype(jnp.bfloat16)
        two.append(begin(ring(part, 1, s2, r2)))
    for part, (s2, r2, s3, r3) in enumerate(((s2_a, r2_a, s3_a, r3_a), (s2_b, r2_b, s3_b, r3_b), (s2_c, r2_c, s3_c, r3_c))):
        arrive(two[part])
        for i in range(4):
            s3[i] = total(part, 1, s2, r2, i)
        three.append(begin(ring(part, 2, s3, r3)))

    for copy in tell_y:
        copy.wait_recv()
    found = jnp.max(row[...] + overs[1, 0] + overs[1, 1] + overs[1, 2])
    any_ref[0] = jnp.where(found > 0.5, 1, 0)

    for part, (s3, r3) in enumerate(((s3_a, r3_a), (s3_b, r3_b), (s3_c, r3_c))):
        arrive(three[part])
        value = s3[place[axes[part][2]]] + r3[0] + r3[1] + r3[2]
        if part < 2:
            done[part, :CUT] = value
        else:
            done[0, CUT:] = value[0]
            done[1, CUT:] = value[1]
    low = lax.broadcasted_iota(jnp.int32, (TILE // 2, 128), 1) < TILE
    for i in range(2):
        even = done[i, pl.ds(0, TILE // 2, stride=2), :]
        odd = done[i, pl.ds(1, TILE // 2, stride=2), :]
        left = jnp.where(low, even, pltpu.roll(odd, 64, 1))
        right = jnp.where(low, pltpu.roll(even, 64, 1), odd)
        for m in range(TILE // 2):
            out_ref[2 * i : 2 * i + 1, m * 128 : (m + 1) * 128] = left[m : m + 1]
            out_ref[2 * i + 1 : 2 * i + 2, m * 128 : (m + 1) * 128] = right[m : m + 1]

    for copies in one + two + three + [tell_x, tell_y]:
        for copy in copies:
            copy.wait_send()
    for r in range(4):
        swap(r).wait_send()
    for t in range(len(others)):
        mu_copy(t, me).wait_send()

    @pl.loop(0, QS)
    def _(q):
        for t in range(len(others)):
            data_copy(q, t, me).wait_send()


def exchange(pool, identity, mu, nu, live, support, coeffs, pair_mu, pair_nu, ints):
    dma = pltpu.SemaphoreType.DMA
    size = SLOTS * TILE
    bf16, f32 = jnp.bfloat16, jnp.float32
    first, second = (CUT, 128), (2, TILE - CUT, 128)

    def rings(lead, kind):
        return [pltpu.VMEM(lead + rest, kind) for rest in (first, first, second)]

    return pl.pallas_call(
        functools.partial(exchange_kernel, pool),
        out_shape=(
            jax.ShapeDtypeStruct((4, TILE * TILE), f32),
            jax.ShapeDtypeStruct((1,), jnp.int32),
        ),
        in_specs=[SMEM] * 3 + [VMEM] * 4 + [pl.BlockSpec(memory_space=pl.ANY)],
        out_specs=(VMEM, SMEM),
        scratch_shapes=[
            pltpu.VMEM((QS, 2, TILE, COLS * N_ORB), bf16),
            pltpu.VMEM((QS, N_ORB - 1, COLS // 128 * pool, 128), bf16),
            pltpu.VMEM((QS, N_ORB, COLS // 128 * pool, 128), bf16),
            pltpu.VMEM((N_ORB, 2 * ROWS, 128), bf16),
            pltpu.VMEM((SUP, OCC, 128), f32),
            pltpu.VMEM((N_ORB, 2 * OCC, 2 * OCC), f32),
            pltpu.VMEM((N_ORB, 2 * OCC, N_ORB * pool), bf16),
            pltpu.VMEM((N_ORB * pool, 128), f32),
            pltpu.VMEM((SLOTS, 128), jnp.int32),
            pltpu.VMEM((4, size // 4, size), f32),
            pltpu.VMEM((size, size), bf16),
            pltpu.VMEM((size, size), bf16),
            pltpu.VMEM((BLOCKS, TILE, 128), bf16),
            pltpu.VMEM((1, pair_mu.shape[1]), jnp.int32),
            pltpu.SMEM((1, pair_mu.shape[1]), jnp.int32),
            pltpu.VMEM((2, 8, 128), jnp.int32),
            pltpu.VMEM((N_ORB, 2, 8, 128), jnp.int32),
            pltpu.VMEM((8, 128), f32),
            pltpu.VMEM((8, 128), f32),
            pltpu.VMEM((2, 3, 8, 128), f32),
            pltpu.VMEM((2, TILE, 128), f32),
            *rings((4, 4, 4), bf16),
            *rings((3, 4, 4), bf16),
            *rings((4, 4), bf16),
            *rings((3, 4), bf16),
            *rings((4,), f32),
            *rings((3,), f32),
            dma((QS,)),
            dma((QS, N_ORB - 1)),
            dma((QS, N_ORB)),
            dma((N_ORB - 1,)),
            dma((N_ORB,)),
            dma((4,)),
            dma((4,)),
            dma(()),
            dma((2, 3)),
            dma((2, 3)),
            dma((9, 3)),
            dma((9, 3)),
        ],
        compiler_params=pltpu.CompilerParams(
            collective_id=identity, has_side_effects=True, vmem_limit_bytes=LIMIT
        ),
        name="exchange",
    )(mu, nu, live, support, coeffs, pair_mu, pair_nu, ints)


def on_device(integrals, tile_mu, tile_nu, live_count, support, coeffs, pair_mu, pair_nu):
    args = (tile_mu, tile_nu, live_count, support.T, coeffs, pair_mu[None, :], pair_nu[None, :], integrals)

    out, over = exchange(POOL, 0, *args)
    return lax.cond(over[0] == 0, lambda: out, lambda: exchange(2 * OCC, 1, *args)[0])


def solution(mesh):
    return jax.shard_map(
        on_device,
        mesh=mesh,
        in_specs=(
            P(("aux", "orb"), None, None),
            P(("aux", "orb")),
            P(("aux", "orb")),
            P(("aux", "orb")),
            P(),
            P(),
            P(),
            P(),
        ),
        out_specs=P(("aux", "orb"), None),
        check_vma=False,
    )
```

```python
import functools

import jax
import jax.numpy as jnp
from jax import lax
from jax.experimental import pallas as pl
from jax.experimental.pallas import tpu as pltpu
from jax.sharding import PartitionSpec as P

TILE = 64
AUX_DEV = 256
OCC = 64
SUP = 16
WT = 32
N_ORB = 8
POOL = 88
SLOTS = 16
QS = 4
COLS = AUX_DEV * TILE // (QS * N_ORB)
ROWS = COLS // 128 * OCC
CUT = 48
MESH = pl.DeviceIdType.MESH
VMEM = pl.BlockSpec(memory_space=pltpu.VMEM)
SMEM = pl.BlockSpec(memory_space=pltpu.SMEM)
LIMIT = 60 * 1024 * 1024

OFFSETS = ((2, 0), (2, 1), (1, 0), (3, 0), (1, 1), (3, 1), (0, 1))


STEPS = (2, 1, 3)
BLOCKS = 17 * 16


def chunk_rows(pool):
    top = pool // 16 * 16
    return top, COLS // 128 * top, COLS // 128 * top + (COLS // 256 * 16 if pool > top else 0)


def exchange_kernel(
    pool,
    mu_ref,
    nu_ref,
    live_ref,
    support_ref,
    coeffs_ref,
    pm_ref,
    pn_ref,
    ints_hbm,
    out_ref,
    any_ref,
    ints,
    sbuf,
    rbuf,
    xbuf,
    tiles,
    unpack,
    merge,
    stack,
    first,
    acc,
    gsend,
    gpeer,
    blocks,
    index,
    index_smem,
    mine,
    mus,
    over,
    row,
    overs,
    done,
    e_a,
    e_b,
    e_c,
    r1_a,
    r1_b,
    r1_c,
    s2_a,
    s2_b,
    s2_c,
    r2_a,
    r2_b,
    r2_c,
    s3_a,
    s3_b,
    s3_c,
    r3_a,
    r3_b,
    r3_c,
    in_sem,
    send_sem,
    recv_sem,
    mu_send,
    mu_recv,
    g_send,
    g_recv,
    index_sem,
    tell_send,
    tell_recv,
    ring_send,
    ring_recv,
):
    top, tops, _ = chunk_rows(pool)
    ragged = pool > top
    aux = lax.axis_index("aux")
    me = lax.axis_index("orb")
    y, x = aux // 4, lax.rem(aux, 4)
    z, core = me // 2, lax.rem(me, 2)
    others = [lax.rem(z + dz, 4) * 2 + lax.rem(core + dc, 2) for dz, dc in OFFSETS]
    peer = others[-1]
    place = {"x": x, "y": y, "z": z}

    def along(axis, step):
        if axis == "x":
            return (y * 4 + lax.rem(x + step, 4), me)
        if axis == "y":
            return (lax.rem(y + step, 4) * 4 + x, me)
        return (aux, lax.rem(z + step, 4) * 2 + core)

    def load(q):
        return pltpu.make_async_copy(
            ints_hbm.at[:, :, pl.ds(pl.multiple_of(q * COLS * N_ORB, COLS * N_ORB), COLS * N_ORB)],
            ints.at[q],
            in_sem.at[q],
        )

    barrier = pltpu.get_barrier_semaphore()
    for other in others:
        pl.semaphore_signal(barrier, inc=1, device_id=(aux, other), device_id_type=MESH)
    for axis in "xy":
        for step in STEPS:
            pl.semaphore_signal(barrier, inc=1, device_id=along(axis, step), device_id_type=MESH)
    for q in range(QS):
        load(q).start()

    lane = lax.broadcasted_iota(jnp.int32, (OCC, 128), 1)
    low = lane < TILE
    one = (
        lax.broadcasted_iota(jnp.int32, (SUP, SUP), 0) == lax.broadcasted_iota(jnp.int32, (SUP, SUP), 1)
    ).astype(jnp.float32)
    support = lax.dot_general(
        support_ref[...].astype(jnp.float32), one, (((0,), (0,)), ((), ())), preferred_element_type=jnp.float32
    )
    halves = []
    for s in range(2):
        total = jnp.zeros((OCC, 128), jnp.float32)
        nu = nu_ref[s].astype(jnp.float32)
        for jj in range(SUP // 2):
            tile = jnp.where(low, support[:, 2 * jj : 2 * jj + 1], support[:, 2 * jj + 1 : 2 * jj + 2])
            block = coeffs_ref[:, jj * 128 : (jj + 1) * 128].astype(jnp.float32)
            total = total + jnp.where(tile == nu, block, 0.0)
        total = total + pltpu.roll(total, 64, 1)
        live = jnp.where(s < live_ref[0], 1.0, 0.0)
        keep = low if s == 0 else jnp.logical_not(low)
        halves.append(jnp.where(keep, total * live, 0.0))
    coef = jnp.concatenate(halves, axis=0).astype(jnp.bfloat16)

    slot = lax.rem(lax.broadcasted_iota(jnp.int32, (8, 128), 0), 2)
    mine[0] = jnp.where(slot < live_ref[0], jnp.where(slot == 0, mu_ref[0], mu_ref[1]), -1)
    mine[1] = jnp.where(slot < live_ref[0], jnp.where(slot == 0, nu_ref[0], nu_ref[1]), -1)

    for j in range(SUP):
        tiles[j] = jnp.broadcast_to(support[:, j : j + 1], (OCC, 128))
    square = (2 * OCC, 2 * OCC)
    to, at = lax.broadcasted_iota(jnp.int32, square, 0), lax.broadcasted_iota(jnp.int32, square, 1)
    before = jnp.where(at < to, 1.0, 0.0).astype(jnp.bfloat16)

    def placement(nus):
        used = []
        for s in range(2):
            nu = nus[s : s + 1].astype(jnp.float32)
            count = jnp.zeros((OCC, 128), jnp.float32)
            for j in range(SUP):
                count = count + jnp.where(tiles[j] == nu, 1.0, 0.0)
            used.append(count)
        used = jnp.concatenate(used, axis=0)
        rank = jnp.dot(before, used.astype(jnp.bfloat16), preferred_element_type=jnp.float32)
        last = slice(2 * OCC - 1, 2 * OCC)
        placed = jnp.where(rank == at.astype(jnp.float32), used, 0.0)
        return placed.astype(jnp.bfloat16), rank[last] + used[last]

    own, _ = placement(mine[1])
    packed = lax.dot_general(own, coef, (((0,), (0,)), ((), ())), preferred_element_type=jnp.float32)
    packed = packed[:pool].astype(jnp.bfloat16)

    def mu_copy(t, device):
        return pltpu.make_async_remote_copy(
            src_ref=mine,
            dst_ref=mus.at[device],
            send_sem=mu_send.at[t],
            recv_sem=mu_recv.at[device],
            device_id=(aux, others[t]),
            device_id_type=MESH,
        )

    def data_copy(q, t, device):
        return pltpu.make_async_remote_copy(
            src_ref=sbuf.at[q, t],
            dst_ref=rbuf.at[q, device],
            send_sem=send_sem.at[q, t],
            recv_sem=recv_sem.at[q, device],
            device_id=(aux, others[t]),
            device_id_type=MESH,
        )

    def swap(r):
        rows = pl.ds(r * 256, 256)
        return pltpu.make_async_remote_copy(
            src_ref=gsend.at[rows],
            dst_ref=gpeer.at[rows],
            send_sem=g_send.at[r],
            recv_sem=g_recv.at[r],
            device_id=(aux, peer),
            device_id_type=MESH,
        )

    def products(q, dest, store):
        block = ints[q, :, :, pl.ds(pl.multiple_of(dest * COLS, COLS), COLS)].reshape(2 * TILE, COLS)
        res = jnp.dot(packed, block, preferred_element_type=jnp.float32)
        for p in range(COLS // 128):
            store(p * top, res[:top, p * 128 : (p + 1) * 128].astype(jnp.bfloat16))
        if ragged:
            for p in range(0, COLS // 128, 2):
                last = [res[top:, (p + i) * 128 : (p + i + 1) * 128] for i in range(2)]
                store(tops + p * 8, jnp.concatenate(last, axis=0).astype(jnp.bfloat16))

    def tell(stage, axis, source):
        return [
            pltpu.make_async_remote_copy(
                src_ref=source,
                dst_ref=overs.at[stage, 3 - step],
                send_sem=tell_send.at[stage, step - 1],
                recv_sem=tell_recv.at[stage, 3 - step],
                device_id=along(axis, step),
                device_id_type=MESH,
            )
            for step in STEPS
        ]

    pl.semaphore_wait(barrier, len(others) + 6)
    for t in range(len(others)):
        mu_copy(t, me).start()

    @pl.loop(0, QS)
    def _(q):
        load(q).wait()
        for t, other in enumerate(others):

            def to_send(row, value):
                sbuf[q, t, row : row + value.shape[0], :] = value

            products(q, other, to_send)
            data_copy(q, t, me).start()

        def to_own(row, value):
            rbuf[q, me, row : row + value.shape[0], :] = value

        products(q, me, to_own)

    mus[me] = mine[...]
    for t, other in enumerate(others):
        mu_copy(t, other).wait_recv()
    over[...] = jnp.zeros_like(over)

    @pl.loop(0, N_ORB)
    def _(source):
        placed, rows = placement(mus[source, 1])
        unpack[source] = placed.astype(jnp.float32).T
        over[...] = jnp.maximum(over[...], jnp.where(rows > pool, 1.0, 0.0))

    tell_x = tell(0, "x", over)
    for copy in tell_x:
        copy.start()

    def mu_of(slot):
        return mus[slot // 2, 0, slot % 2 : slot % 2 + 1]

    for s in range(SLOTS):
        is_first = jnp.ones((1, 128), jnp.int32)
        for t in range(s):
            is_first = jnp.where(mu_of(t) == mu_of(s), 0, is_first)
        first[s : s + 1] = jnp.where(mu_of(s) >= 0, is_first, 0)
    low_row = low[:1]
    if ragged:
        stack[N_ORB * top :] = jnp.zeros((N_ORB * 16, 128), jnp.float32)
    for pair in range(N_ORB):

        @pl.loop(0, N_ORB)
        def _(source):
            def shares(slot, s):
                same = mus[source, 0, s : s + 1] == mu_of(slot)
                return jnp.where(same, first[slot : slot + 1], 0).astype(jnp.float32)

            kept = jnp.where(low_row, shares(2 * pair, 0), shares(2 * pair + 1, 1))
            turned = jnp.where(low_row, shares(2 * pair, 1), shares(2 * pair + 1, 0))
            placed = unpack[source]
            both = placed * kept + pltpu.roll(placed, 64, 1) * turned
            stack[pl.ds(pl.multiple_of(source * top, top), top)] = both[:top]
            if ragged:
                stack[pl.ds(pl.multiple_of(N_ORB * top + source * 16, 16), 8)] = both[top:pool]

        merged = stack[...].T
        at = slice(pair % 4 * 128, (pair % 4 + 1) * 128)
        merge[0, pair // 4, at] = merged.astype(jnp.bfloat16)
        if ragged:
            turned = pltpu.roll(merged[:, N_ORB * top :], 8, 1)
            merged = jnp.concatenate([merged[:, : N_ORB * top], turned], axis=1)
            merge[1, pair // 4, at] = merged.astype(jnp.bfloat16)

    k = lax.broadcasted_iota(jnp.int32, pm_ref.shape, 1)
    u = jnp.full(pm_ref.shape, SLOTS, jnp.int32)
    v = jnp.full(pm_ref.shape, -1, jnp.int32)
    for s in range(SLOTS):
        known = first[s : s + 1, :1] > 0
        tile = mu_of(s)[:, :1]
        u = jnp.where(jnp.logical_and(known, pm_ref[...] == tile), s, u)
        v = jnp.where(jnp.logical_and(known, pn_ref[...] == tile), s, v)
    u = jnp.where(v >= 0, u, SLOTS)
    v = jnp.maximum(v, 0)
    index[...] = (((v + k) & 1) * 8 + (v >> 1)) * 17 + u
    to_smem = pltpu.make_async_copy(index, index_smem, index_sem)
    to_smem.start()
    for c in range(16):
        blocks[c * 17 + 16] = jnp.zeros((TILE, 128), jnp.bfloat16)

    for copy in tell_x:
        copy.wait_recv()
    row[...] = over[...] + overs[0, 0] + overs[0, 1] + overs[0, 2]
    tell_y = tell(1, "y", row)
    for copy in tell_y:
        copy.start()

    acc[...] = jnp.zeros_like(acc)

    def spread(q):
        def column(p):
            parts = [rbuf[q, source, p * top : (p + 1) * top] for source in range(N_ORB)]
            if ragged:
                at = tops + p // 2 * 16
                parts += [rbuf[q, source, at : at + 16] for source in range(N_ORB)]
            return jnp.concatenate(parts, axis=0)

        for odd_p in range(2):
            data = jnp.concatenate([column(p) for p in range(odd_p, COLS // 128, 2)], axis=1)
            for half in range(2):
                res = jnp.dot(merge[odd_p if ragged else 0, half], data, preferred_element_type=jnp.float32)
                for n, p in enumerate(range(odd_p, COLS // 128, 2)):
                    lanes = slice(n * 128, (n + 1) * 128)
                    for i in range(4):
                        a = res[i * 128 : i * 128 + OCC, lanes]
                        b = res[i * 128 + OCC : (i + 1) * 128, lanes]
                        even = jnp.where(low, a, pltpu.roll(b, 64, 1))
                        odd = jnp.where(low, pltpu.roll(a, 64, 1), b)
                        xbuf[half * 4 + i, p * OCC : (p + 1) * OCC] = even.astype(jnp.bfloat16)
                        xbuf[half * 4 + i, ROWS + p * OCC : ROWS + (p + 1) * OCC] = odd.astype(jnp.bfloat16)

    def gram(r):
        left = jnp.concatenate([xbuf[2 * r], xbuf[2 * r + 1]], axis=1)
        for c in range(4):
            right = jnp.concatenate([xbuf[2 * c], xbuf[2 * c + 1]], axis=1)
            acc[r, :, c * 256 : (c + 1) * 256] += lax.dot_general(
                left, right, (((0,), (0,)), ((), ())), preferred_element_type=jnp.float32
            )

    @pl.loop(0, QS)
    def _(q):
        for t, other in enumerate(others):
            data_copy(q, t, other).wait_recv()
        spread(q)

        @pl.when(q < QS - 1)
        def _():
            @pl.loop(0, 4)
            def _(r):
                gram(r)

    for r in range(4):
        gram(r)
        gsend[r * 256 : (r + 1) * 256] = acc[r].astype(jnp.bfloat16)
        swap(r).start()
    for r in range(4):
        swap(r).wait_recv()
        for c in range(8):
            lanes = slice(c * 128, (c + 1) * 128)
            total = acc[r, :, lanes] + gpeer[r * 256 : (r + 1) * 256, lanes].astype(jnp.float32)
            turned = pltpu.roll(total, 64, 1)
            for i in range(4):
                rows = slice(i * TILE, (i + 1) * TILE)
                blocks[c * 17 + r * 4 + i] = total[rows].astype(jnp.bfloat16)
                blocks[(8 + c) * 17 + r * 4 + i] = turned[rows].astype(jnp.bfloat16)

    to_smem.wait()

    def block(yy, xx, zz, j):
        k = (yy * 4 + xx) * 32 + zz * 8 + core * 4 + 2 * j
        return jnp.where(low, blocks[index_smem[0, k]], blocks[index_smem[0, k + 1]])

    axes = ("xyz", "yzx", "zxy")

    def ring(part, stage, source, landing, steps=STEPS):
        axis = axes[part][stage]
        at = part * 3 + stage
        return [
            pltpu.make_async_remote_copy(
                src_ref=source.at[lax.rem(place[axis] + step, 4)],
                dst_ref=landing.at[3 - step],
                send_sem=ring_send.at[at, step - 1],
                recv_sem=ring_recv.at[at, 3 - step],
                device_id=along(axis, step),
                device_id_type=MESH,
            )
            for step in steps
        ]

    def begin(copies):
        for copy in copies:
            copy.start()
        return copies

    def arrive(copies):
        for copy in copies:
            copy.wait_recv()

    everything = []
    one = [[], [], []]
    for step in STEPS + (0,):
        xx = lax.rem(x + step, 4)

        @pl.loop(0, 16)
        def _(i):
            yy, zz = i // 4, lax.rem(i, 4)
            value = block(yy, xx, zz, 0)
            e_a[xx, yy, zz] = value[:CUT]
            e_c[zz, xx, yy, 0] = value[CUT:]

        if step:
            one[0] += begin(ring(0, 0, e_a, r1_a, (step,)))
        yy = lax.rem(y + step, 4)

        @pl.loop(0, 16)
        def _(i):
            zz, xx = i // 4, lax.rem(i, 4)
            value = block(yy, xx, zz, 1)
            e_b[yy, zz, xx] = value[:CUT]
            e_c[zz, xx, yy, 1] = value[CUT:]

        if step:
            one[1] += begin(ring(1, 0, e_b, r1_b, (step,)))
    one[2] = begin(ring(2, 0, e_c, r1_c))

    def total(part, stage, source, landing, i):
        at = place[axes[part][stage]]
        value = source[at, i].astype(jnp.float32)
        for n in range(3):
            value = value + landing[n, i].astype(jnp.float32)
        return value

    two, three = [], []
    for part, (e, r1, s2, r2) in enumerate(((e_a, r1_a, s2_a, r2_a), (e_b, r1_b, s2_b, r2_b), (e_c, r1_c, s2_c, r2_c))):
        arrive(one[part])
        for i in range(4):
            s2[i] = total(part, 0, e, r1, i).astype(jnp.bfloat16)
        two.append(begin(ring(part, 1, s2, r2)))
    for part, (s2, r2, s3, r3) in enumerate(((s2_a, r2_a, s3_a, r3_a), (s2_b, r2_b, s3_b, r3_b), (s2_c, r2_c, s3_c, r3_c))):
        arrive(two[part])
        for i in range(4):
            s3[i] = total(part, 1, s2, r2, i)
        three.append(begin(ring(part, 2, s3, r3)))

    for copy in tell_y:
        copy.wait_recv()
    found = jnp.max(row[...] + overs[1, 0] + overs[1, 1] + overs[1, 2])
    any_ref[0] = jnp.where(found > 0.5, 1, 0)

    for part, (s3, r3) in enumerate(((s3_a, r3_a), (s3_b, r3_b), (s3_c, r3_c))):
        arrive(three[part])
        value = s3[place[axes[part][2]]] + r3[0] + r3[1] + r3[2]
        if part < 2:
            done[part, :CUT] = value
        else:
            done[0, CUT:] = value[0]
            done[1, CUT:] = value[1]
    low = lax.broadcasted_iota(jnp.int32, (TILE // 2, 128), 1) < TILE
    for i in range(2):
        even = done[i, pl.ds(0, TILE // 2, stride=2), :]
        odd = done[i, pl.ds(1, TILE // 2, stride=2), :]
        left = jnp.where(low, even, pltpu.roll(odd, 64, 1))
        right = jnp.where(low, pltpu.roll(even, 64, 1), odd)
        for m in range(TILE // 2):
            out_ref[2 * i : 2 * i + 1, m * 128 : (m + 1) * 128] = left[m : m + 1]
            out_ref[2 * i + 1 : 2 * i + 2, m * 128 : (m + 1) * 128] = right[m : m + 1]

    for copies in one + two + three + [tell_x, tell_y]:
        for copy in copies:
            copy.wait_send()
    for r in range(4):
        swap(r).wait_send()
    for t in range(len(others)):
        mu_copy(t, me).wait_send()

    @pl.loop(0, QS)
    def _(q):
        for t in range(len(others)):
            data_copy(q, t, me).wait_send()


def exchange(pool, identity, mu, nu, live, support, coeffs, pair_mu, pair_nu, ints):
    top, _, rows = chunk_rows(pool)
    depth = N_ORB * (top + (16 if pool > top else 0))
    dma = pltpu.SemaphoreType.DMA
    size = SLOTS * TILE
    bf16, f32 = jnp.bfloat16, jnp.float32
    first, second = (CUT, 128), (2, TILE - CUT, 128)

    def rings(lead, kind):
        return [pltpu.VMEM(lead + rest, kind) for rest in (first, first, second)]

    return pl.pallas_call(
        functools.partial(exchange_kernel, pool),
        out_shape=(
            jax.ShapeDtypeStruct((4, TILE * TILE), f32),
            jax.ShapeDtypeStruct((1,), jnp.int32),
        ),
        in_specs=[SMEM] * 3 + [VMEM] * 4 + [pl.BlockSpec(memory_space=pl.ANY)],
        out_specs=(VMEM, SMEM),
        scratch_shapes=[
            pltpu.VMEM((QS, 2, TILE, COLS * N_ORB), bf16),
            pltpu.VMEM((QS, N_ORB - 1, rows, 128), bf16),
            pltpu.VMEM((QS, N_ORB, rows, 128), bf16),
            pltpu.VMEM((N_ORB, 2 * ROWS, 128), bf16),
            pltpu.VMEM((SUP, OCC, 128), f32),
            pltpu.VMEM((N_ORB, 2 * OCC, 2 * OCC), f32),
            pltpu.VMEM((2 if pool > top else 1, 2, 8 * OCC, depth), bf16),
            pltpu.VMEM((depth, 128), f32),
            pltpu.VMEM((SLOTS, 128), jnp.int32),
            pltpu.VMEM((4, size // 4, size), f32),
            pltpu.VMEM((size, size), bf16),
            pltpu.VMEM((size, size), bf16),
            pltpu.VMEM((BLOCKS, TILE, 128), bf16),
            pltpu.VMEM((1, pair_mu.shape[1]), jnp.int32),
            pltpu.SMEM((1, pair_mu.shape[1]), jnp.int32),
            pltpu.VMEM((2, 8, 128), jnp.int32),
            pltpu.VMEM((N_ORB, 2, 8, 128), jnp.int32),
            pltpu.VMEM((8, 128), f32),
            pltpu.VMEM((8, 128), f32),
            pltpu.VMEM((2, 3, 8, 128), f32),
            pltpu.VMEM((2, TILE, 128), f32),
            *rings((4, 4, 4), bf16),
            *rings((3, 4, 4), bf16),
            *rings((4, 4), bf16),
            *rings((3, 4), bf16),
            *rings((4,), f32),
            *rings((3,), f32),
            dma((QS,)),
            dma((QS, N_ORB - 1)),
            dma((QS, N_ORB)),
            dma((N_ORB - 1,)),
            dma((N_ORB,)),
            dma((4,)),
            dma((4,)),
            dma(()),
            dma((2, 3)),
            dma((2, 3)),
            dma((9, 3)),
            dma((9, 3)),
        ],
        compiler_params=pltpu.CompilerParams(
            collective_id=identity, has_side_effects=True, vmem_limit_bytes=LIMIT
        ),
        name="exchange",
    )(mu, nu, live, support, coeffs, pair_mu, pair_nu, ints)


def on_device(integrals, tile_mu, tile_nu, live_count, support, coeffs, pair_mu, pair_nu):
    args = (tile_mu, tile_nu, live_count, support.T, coeffs, pair_mu[None, :], pair_nu[None, :], integrals)

    out, over = exchange(POOL, 0, *args)
    return lax.cond(over[0] == 0, lambda: out, lambda: exchange(2 * OCC, 1, *args)[0])


def solution(mesh):
    return jax.shard_map(
        on_device,
        mesh=mesh,
        in_specs=(
            P(("aux", "orb"), None, None),
            P(("aux", "orb")),
            P(("aux", "orb")),
            P(("aux", "orb")),
            P(),
            P(),
            P(),
            P(),
        ),
        out_specs=P(("aux", "orb"), None),
        check_vma=False,
    )
```

```python
import functools

import jax
import jax.numpy as jnp
from jax import lax
from jax.experimental import pallas as pl
from jax.experimental.pallas import tpu as pltpu
from jax.sharding import PartitionSpec as P

TILE = 64
AUX_DEV = 256
OCC = 64
SUP = 16
WT = 32
N_ORB = 8
POOL = 88
NPAIR = 512
SLOTS = 16
QS = 4
COLS = AUX_DEV * TILE // (QS * N_ORB)
ROWS = COLS // 128 * OCC
CAP = 20
MESH = pl.DeviceIdType.MESH
VMEM = pl.BlockSpec(memory_space=pltpu.VMEM)
SMEM = pl.BlockSpec(memory_space=pltpu.SMEM)
LIMIT = 60 * 1024 * 1024

OFFSETS = ((2, 0), (2, 1), (1, 0), (3, 0), (1, 1), (3, 1), (0, 1))


STEPS = (2, 1, 3)


def chunk_rows(pool):
    top = pool // 16 * 16
    return top, COLS // 128 * top, COLS // 128 * top + (COLS // 256 * 16 if pool > top else 0)


def exchange_kernel(
    pool,
    cap,
    mu_ref,
    nu_ref,
    live_ref,
    support_ref,
    coeffs_ref,
    pm_ref,
    pn_ref,
    ints_hbm,
    out_ref,
    any_ref,
    ints,
    sbuf,
    rbuf,
    xbuf,
    tiles,
    unpack,
    merge,
    stack,
    first,
    acc,
    order,
    index,
    order_smem,
    index_smem,
    mine,
    mus,
    over,
    row,
    overs,
    done,
    gsend,
    gpeer,
    kept_tiles,
    sz,
    rz,
    blocks,
    e_a,
    e_b,
    r1_a,
    r1_b,
    s2_a,
    s2_b,
    r2_a,
    r2_b,
    in_sem,
    send_sem,
    recv_sem,
    mu_send,
    mu_recv,
    g_send,
    g_recv,
    order_sem,
    index_sem,
    tell_send,
    tell_recv,
    ring_send,
    ring_recv,
):
    top, tops, _ = chunk_rows(pool)
    ragged = pool > top
    lists = order.shape[1]
    aux = lax.axis_index("aux")
    me = lax.axis_index("orb")
    y, x = aux // 4, lax.rem(aux, 4)
    z, core = me // 2, lax.rem(me, 2)
    others = [lax.rem(z + dz, 4) * 2 + lax.rem(core + dc, 2) for dz, dc in OFFSETS]
    peer = others[-1]
    place = {"x": x, "y": y, "z": z}

    def along(axis, step):
        if axis == "x":
            return (y * 4 + lax.rem(x + step, 4), me)
        if axis == "y":
            return (lax.rem(y + step, 4) * 4 + x, me)
        return (aux, lax.rem(z + step, 4) * 2 + core)

    def load(q):
        return pltpu.make_async_copy(
            ints_hbm.at[:, :, pl.ds(pl.multiple_of(q * COLS * N_ORB, COLS * N_ORB), COLS * N_ORB)],
            ints.at[q],
            in_sem.at[q],
        )

    barrier = pltpu.get_barrier_semaphore()
    for other in others:
        pl.semaphore_signal(barrier, inc=1, device_id=(aux, other), device_id_type=MESH)
    for axis in "xy":
        for step in STEPS:
            pl.semaphore_signal(barrier, inc=1, device_id=along(axis, step), device_id_type=MESH)
    for q in range(QS):
        load(q).start()

    lane = lax.broadcasted_iota(jnp.int32, (OCC, 128), 1)
    low = lane < TILE
    one = (
        lax.broadcasted_iota(jnp.int32, (SUP, SUP), 0) == lax.broadcasted_iota(jnp.int32, (SUP, SUP), 1)
    ).astype(jnp.float32)
    support = lax.dot_general(
        support_ref[...].astype(jnp.float32), one, (((0,), (0,)), ((), ())), preferred_element_type=jnp.float32
    )
    halves = []
    for s in range(2):
        total = jnp.zeros((OCC, 128), jnp.float32)
        nu = nu_ref[s].astype(jnp.float32)
        for jj in range(SUP // 2):
            tile = jnp.where(low, support[:, 2 * jj : 2 * jj + 1], support[:, 2 * jj + 1 : 2 * jj + 2])
            block = coeffs_ref[:, jj * 128 : (jj + 1) * 128].astype(jnp.float32)
            total = total + jnp.where(tile == nu, block, 0.0)
        total = total + pltpu.roll(total, 64, 1)
        live = jnp.where(s < live_ref[0], 1.0, 0.0)
        keep = low if s == 0 else jnp.logical_not(low)
        halves.append(jnp.where(keep, total * live, 0.0))
    coef = jnp.concatenate(halves, axis=0).astype(jnp.bfloat16)

    slot = lax.rem(lax.broadcasted_iota(jnp.int32, (8, 128), 0), 2)
    mine[0] = jnp.where(slot < live_ref[0], jnp.where(slot == 0, mu_ref[0], mu_ref[1]), -1)
    mine[1] = jnp.where(slot < live_ref[0], jnp.where(slot == 0, nu_ref[0], nu_ref[1]), -1)

    for j in range(SUP):
        tiles[j] = jnp.broadcast_to(support[:, j : j + 1], (OCC, 128))
    square = (2 * OCC, 2 * OCC)
    to, at = lax.broadcasted_iota(jnp.int32, square, 0), lax.broadcasted_iota(jnp.int32, square, 1)
    before = jnp.where(at < to, 1.0, 0.0).astype(jnp.bfloat16)

    def placement(nus):
        used = []
        for s in range(2):
            nu = nus[s : s + 1].astype(jnp.float32)
            count = jnp.zeros((OCC, 128), jnp.float32)
            for j in range(SUP):
                count = count + jnp.where(tiles[j] == nu, 1.0, 0.0)
            used.append(count)
        used = jnp.concatenate(used, axis=0)
        rank = jnp.dot(before, used.astype(jnp.bfloat16), preferred_element_type=jnp.float32)
        last = slice(2 * OCC - 1, 2 * OCC)
        placed = jnp.where(rank == at.astype(jnp.float32), used, 0.0)
        return placed.astype(jnp.bfloat16), rank[last] + used[last]

    own, _ = placement(mine[1])
    packed = lax.dot_general(own, coef, (((0,), (0,)), ((), ())), preferred_element_type=jnp.float32)
    packed = packed[:pool].astype(jnp.bfloat16)

    def mu_copy(t, device):
        return pltpu.make_async_remote_copy(
            src_ref=mine,
            dst_ref=mus.at[device],
            send_sem=mu_send.at[t],
            recv_sem=mu_recv.at[device],
            device_id=(aux, others[t]),
            device_id_type=MESH,
        )

    def data_copy(q, t, device):
        return pltpu.make_async_remote_copy(
            src_ref=sbuf.at[q, t],
            dst_ref=rbuf.at[q, device],
            send_sem=send_sem.at[q, t],
            recv_sem=recv_sem.at[q, device],
            device_id=(aux, others[t]),
            device_id_type=MESH,
        )

    def swap(step):
        zz = lax.rem(z + step, 4)
        return pltpu.make_async_remote_copy(
            src_ref=gsend.at[zz],
            dst_ref=gpeer.at[zz],
            send_sem=g_send.at[step],
            recv_sem=g_recv.at[step],
            device_id=(aux, peer),
            device_id_type=MESH,
        )

    def products(q, dest, store):
        block = ints[q, :, :, pl.ds(pl.multiple_of(dest * COLS, COLS), COLS)].reshape(2 * TILE, COLS)
        res = jnp.dot(packed, block, preferred_element_type=jnp.float32)
        for p in range(COLS // 128):
            store(p * top, res[:top, p * 128 : (p + 1) * 128].astype(jnp.bfloat16))
        if ragged:
            for p in range(0, COLS // 128, 2):
                last = [res[top:, (p + i) * 128 : (p + i + 1) * 128] for i in range(2)]
                store(tops + p * 8, jnp.concatenate(last, axis=0).astype(jnp.bfloat16))

    def tell(stage, axis, source):
        return [
            pltpu.make_async_remote_copy(
                src_ref=source,
                dst_ref=overs.at[stage, 3 - step],
                send_sem=tell_send.at[stage, step - 1],
                recv_sem=tell_recv.at[stage, 3 - step],
                device_id=along(axis, step),
                device_id_type=MESH,
            )
            for step in STEPS
        ]

    pl.semaphore_wait(barrier, len(others) + 6)
    for t in range(len(others)):
        mu_copy(t, me).start()

    @pl.loop(0, QS)
    def _(q):
        load(q).wait()
        for t, other in enumerate(others):

            def to_send(row, value):
                sbuf[q, t, row : row + value.shape[0], :] = value

            products(q, other, to_send)
            data_copy(q, t, me).start()

        def to_own(row, value):
            rbuf[q, me, row : row + value.shape[0], :] = value

        products(q, me, to_own)

    mus[me] = mine[...]
    for t, other in enumerate(others):
        mu_copy(t, other).wait_recv()
    over[...] = jnp.zeros_like(over)

    @pl.loop(0, N_ORB)
    def _(source):
        placed, rows = placement(mus[source, 1])
        unpack[source] = placed.astype(jnp.float32).T
        over[...] = jnp.maximum(over[...], jnp.where(rows > pool, 1.0, 0.0))

    def mu_of(slot):
        return mus[slot // 2, 0, slot % 2 : slot % 2 + 1]

    for s in range(SLOTS):
        is_first = jnp.ones((1, 128), jnp.int32)
        for t in range(s):
            is_first = jnp.where(mu_of(t) == mu_of(s), 0, is_first)
        first[s : s + 1] = jnp.where(mu_of(s) >= 0, is_first, 0)
    low_row = low[:1]
    if ragged:
        stack[N_ORB * top :] = jnp.zeros((N_ORB * 16, 128), jnp.float32)
    for pair in range(N_ORB):

        @pl.loop(0, N_ORB)
        def _(source):
            def shares(slot, s):
                same = mus[source, 0, s : s + 1] == mu_of(slot)
                return jnp.where(same, first[slot : slot + 1], 0).astype(jnp.float32)

            kept = jnp.where(low_row, shares(2 * pair, 0), shares(2 * pair + 1, 1))
            turned = jnp.where(low_row, shares(2 * pair, 1), shares(2 * pair + 1, 0))
            placed = unpack[source]
            both = placed * kept + pltpu.roll(placed, 64, 1) * turned
            stack[pl.ds(pl.multiple_of(source * top, top), top)] = both[:top]
            if ragged:
                stack[pl.ds(pl.multiple_of(N_ORB * top + source * 16, 16), 8)] = both[top:pool]

        merged = stack[...].T
        at = slice(pair % 4 * 128, (pair % 4 + 1) * 128)
        merge[0, pair // 4, at] = merged.astype(jnp.bfloat16)
        if ragged:
            turned = pltpu.roll(merged[:, N_ORB * top :], 8, 1)
            merged = jnp.concatenate([merged[:, : N_ORB * top], turned], axis=1)
            merge[1, pair // 4, at] = merged.astype(jnp.bfloat16)

    k = lax.broadcasted_iota(jnp.int32, pm_ref.shape, 1)
    u = jnp.full(pm_ref.shape, -1, jnp.int32)
    v = jnp.full(pm_ref.shape, -1, jnp.int32)
    for s in range(SLOTS):
        known = first[s : s + 1, :1] > 0
        tile = mu_of(s)[:, :1]
        u = jnp.where(jnp.logical_and(known, pm_ref[...] == tile), s, u)
        v = jnp.where(jnp.logical_and(known, pn_ref[...] == tile), s, v)
    active = jnp.logical_and(u >= 0, v >= 0)
    npair = pm_ref.shape[1]
    square = (npair, npair)
    to, at = lax.broadcasted_iota(jnp.int32, square, 0), lax.broadcasted_iota(jnp.int32, square, 1)
    ahead = jnp.where(jnp.logical_and(to < at, ((to ^ at) & 28) == 0), 1.0, 0.0).astype(jnp.bfloat16)
    flags = jnp.broadcast_to(jnp.where(active, 1.0, 0.0), (8, npair)).astype(jnp.bfloat16)
    rank = jnp.dot(flags, ahead, preferred_element_type=jnp.float32)[:1].astype(jnp.int32)
    spill = jnp.logical_and(active, rank >= cap)
    over[...] = jnp.maximum(over[...], jnp.max(jnp.where(spill, 1.0, 0.0)))
    listed = jnp.logical_and(active, rank < cap)
    at_list = jnp.where(listed, ((k >> 2) & 7) * cap + rank, -1)
    chosen = jnp.where(lax.broadcasted_iota(jnp.int32, (lists, npair), 0) == at_list, 1.0, 0.0)
    tiles_of = jnp.broadcast_to((u * SLOTS + v).astype(jnp.float32), (8, npair)).astype(jnp.bfloat16)
    order[...] = lax.dot_general(
        tiles_of, chosen.astype(jnp.bfloat16), (((1,), (1,)), ((), ())), preferred_element_type=jnp.float32
    )[:1].astype(jnp.int32)
    index[...] = jnp.where(listed, ((rank + k) & 1) * (cap // 2 + 1) + (rank >> 1), cap // 2)
    to_smem = [
        pltpu.make_async_copy(order, order_smem, order_sem),
        pltpu.make_async_copy(index, index_smem, index_sem),
    ]
    for copy in to_smem:
        copy.start()
    blocks[cap // 2] = jnp.zeros((TILE, 128), jnp.bfloat16)

    tell_x = tell(0, "x", over)
    for copy in tell_x:
        copy.start()
    for copy in tell_x:
        copy.wait_recv()
    row[...] = over[...] + overs[0, 0] + overs[0, 1] + overs[0, 2]
    tell_y = tell(1, "y", row)
    for copy in tell_y:
        copy.start()

    acc[...] = jnp.zeros_like(acc)

    def spread(q):
        def column(p):
            parts = [rbuf[q, source, p * top : (p + 1) * top] for source in range(N_ORB)]
            if ragged:
                at = tops + p // 2 * 16
                parts += [rbuf[q, source, at : at + 16] for source in range(N_ORB)]
            return jnp.concatenate(parts, axis=0)

        for odd_p in range(2):
            data = jnp.concatenate([column(p) for p in range(odd_p, COLS // 128, 2)], axis=1)
            for half in range(2):
                res = jnp.dot(merge[odd_p if ragged else 0, half], data, preferred_element_type=jnp.float32)
                for n, p in enumerate(range(odd_p, COLS // 128, 2)):
                    lanes = slice(n * 128, (n + 1) * 128)
                    for i in range(4):
                        a = res[i * 128 : i * 128 + OCC, lanes]
                        b = res[i * 128 + OCC : (i + 1) * 128, lanes]
                        even = jnp.where(low, a, pltpu.roll(b, 64, 1))
                        odd = jnp.where(low, pltpu.roll(a, 64, 1), b)
                        xbuf[half * 4 + i, p * OCC : (p + 1) * OCC] = even.astype(jnp.bfloat16)
                        xbuf[half * 4 + i, ROWS + p * OCC : ROWS + (p + 1) * OCC] = odd.astype(jnp.bfloat16)

    def gram(r):
        left = jnp.concatenate([xbuf[2 * r], xbuf[2 * r + 1]], axis=1)
        for c in range(4):
            right = jnp.concatenate([xbuf[2 * c], xbuf[2 * c + 1]], axis=1)
            res = lax.dot_general(
                left, right, (((0,), (0,)), ((), ())), preferred_element_type=jnp.float32
            )
            for i in range(4):
                for h in range(2):
                    acc[(r * 4 + i) * 8 + c * 2 + h] += res[i * TILE : (i + 1) * TILE, h * 128 : (h + 1) * 128]

    @pl.loop(0, QS)
    def _(q):
        for t, other in enumerate(others):
            data_copy(q, t, other).wait_recv()
        spread(q)

        @pl.loop(0, 4)
        def _(r):
            gram(r)

    for copy in to_smem:
        copy.wait()

    def ring(part, stage, axis, source, landing, step):
        at = part * 2 + stage
        return pltpu.make_async_remote_copy(
            src_ref=source.at[lax.rem(place[axis] + step, 4)],
            dst_ref=landing.at[3 - step],
            send_sem=ring_send.at[at, step - 1],
            recv_sem=ring_recv.at[at, 3 - step],
            device_id=along(axis, step),
            device_id_type=MESH,
        )

    def started(copy):
        copy.start()
        return copy

    def packed_tiles(owner, b):
        at = owner * cap + 2 * b
        t0, t1 = order_smem[0, at] & 255, order_smem[0, at + 1] & 255
        tile0, tile1 = acc[t0 >> 1], acc[t1 >> 1]
        in_place = jnp.broadcast_to(jnp.where(low_row, t0 & 1, 1 - (t1 & 1)), low.shape) == 0
        straight, crossed = jnp.where(low, tile0, tile1), jnp.where(low, tile1, tile0)
        return jnp.where(in_place, straight, pltpu.roll(crossed, 64, 1))

    unroll = 10 if cap % 10 == 0 else 4

    def give(step):
        zz = lax.rem(z + step, 4)

        @pl.loop(0, cap // 2, unroll=unroll)
        def _(b):
            gsend[zz, b] = packed_tiles(zz * 2 + 1 - core, b).astype(jnp.bfloat16)

        swap(step).start()

    z_copies = []

    def take(step):
        zz = lax.rem(z + step, 4)

        @pl.loop(0, cap // 2, unroll=unroll)
        def _(b):
            kept_tiles[b] = packed_tiles(zz * 2 + core, b)

        swap(step).wait_recv()
        sz[zz] = (kept_tiles[...] + gpeer[zz].astype(jnp.float32)).astype(jnp.bfloat16)
        if step:
            z_copies.append(started(ring(2, 0, "z", sz, rz, step)))

    turns = STEPS + (0,)
    give(turns[0])
    for i in range(4):
        if i < 3:
            give(turns[i + 1])
        take(turns[i])

    for copy in z_copies:
        copy.wait_recv()
    for b in range(cap // 2):
        total = sz[z, b].astype(jnp.float32)
        for n in range(3):
            total = total + rz[n, b].astype(jnp.float32)
        blocks[b] = total.astype(jnp.bfloat16)
        blocks[cap // 2 + 1 + b] = pltpu.roll(total, 64, 1).astype(jnp.bfloat16)

    def block(yy, xx, j):
        k = (yy * 4 + xx) * 32 + z * 8 + core * 4 + 2 * j
        left, right = (jnp.clip(index_smem[0, k + h], 0, cap + 1) for h in range(2))
        return jnp.where(low, blocks[left], blocks[right])

    one_a, one_b = [], []
    for step in turns:
        xx, yy = lax.rem(x + step, 4), lax.rem(y + step, 4)
        for i in range(4):
            e_a[xx, i] = block(i, xx, 0)
        if step:
            one_a.append(started(ring(0, 0, "x", e_a, r1_a, step)))
        for i in range(4):
            e_b[yy, i] = block(yy, i, 1)
        if step:
            one_b.append(started(ring(1, 0, "y", e_b, r1_b, step)))

    two = []
    for part, copies, axis, then, e, r1, s2, r2 in (
        (0, one_a, "x", "y", e_a, r1_a, s2_a, r2_a),
        (1, one_b, "y", "x", e_b, r1_b, s2_b, r2_b),
    ):
        for copy in copies:
            copy.wait_recv()
        for step in turns:
            i = lax.rem(place[then] + step, 4)
            total = e[place[axis], i].astype(jnp.float32)
            for n in range(3):
                total = total + r1[n, i].astype(jnp.float32)
            s2[i] = total
            if step:
                two.append(started(ring(part, 1, then, s2, r2, step)))

    for copy in tell_y:
        copy.wait_recv()
    found = jnp.max(row[...] + overs[1, 0] + overs[1, 1] + overs[1, 2])
    any_ref[0] = jnp.where(found > 0.5, 1, 0)

    for part, then, s2, r2 in ((0, "y", s2_a, r2_a), (1, "x", s2_b, r2_b)):
        for copy in two[part * 3 : part * 3 + 3]:
            copy.wait_recv()
        done[part] = s2[place[then]] + r2[0] + r2[1] + r2[2]
    low = lax.broadcasted_iota(jnp.int32, (TILE // 2, 128), 1) < TILE
    for i in range(2):
        even = done[i, pl.ds(0, TILE // 2, stride=2), :]
        odd = done[i, pl.ds(1, TILE // 2, stride=2), :]
        left = jnp.where(low, even, pltpu.roll(odd, 64, 1))
        right = jnp.where(low, pltpu.roll(even, 64, 1), odd)
        for m in range(TILE // 2):
            out_ref[2 * i : 2 * i + 1, m * 128 : (m + 1) * 128] = left[m : m + 1]
            out_ref[2 * i + 1 : 2 * i + 2, m * 128 : (m + 1) * 128] = right[m : m + 1]

    for copy in z_copies + one_a + one_b + two + tell_x + tell_y:
        copy.wait_send()
    for step in range(4):
        swap(step).wait_send()
    for t in range(len(others)):
        mu_copy(t, me).wait_send()

    @pl.loop(0, QS)
    def _(q):
        for t in range(len(others)):
            data_copy(q, t, me).wait_send()


def exchange(pool, cap, identity, mu, nu, live, support, coeffs, pair_mu, pair_nu, ints):
    top, _, rows = chunk_rows(pool)
    depth = N_ORB * (top + (16 if pool > top else 0))
    dma = pltpu.SemaphoreType.DMA
    bf16, f32 = jnp.bfloat16, jnp.float32
    half = cap // 2
    lists = pl.cdiv(N_ORB * cap, 128) * 128

    return pl.pallas_call(
        functools.partial(exchange_kernel, pool, cap),
        out_shape=(
            jax.ShapeDtypeStruct((4, TILE * TILE), f32),
            jax.ShapeDtypeStruct((1,), jnp.int32),
        ),
        in_specs=[SMEM] * 3 + [VMEM] * 4 + [pl.BlockSpec(memory_space=pl.ANY)],
        out_specs=(VMEM, SMEM),
        scratch_shapes=[
            pltpu.VMEM((QS, 2, TILE, COLS * N_ORB), bf16),
            pltpu.VMEM((QS, N_ORB - 1, rows, 128), bf16),
            pltpu.VMEM((QS, N_ORB, rows, 128), bf16),
            pltpu.VMEM((N_ORB, 2 * ROWS, 128), bf16),
            pltpu.VMEM((SUP, OCC, 128), f32),
            pltpu.VMEM((N_ORB, 2 * OCC, 2 * OCC), f32),
            pltpu.VMEM((2 if pool > top else 1, 2, 8 * OCC, depth), bf16),
            pltpu.VMEM((depth, 128), f32),
            pltpu.VMEM((SLOTS, 128), jnp.int32),
            pltpu.VMEM((SLOTS * SLOTS // 2, TILE, 128), f32),
            pltpu.VMEM((1, lists), jnp.int32),
            pltpu.VMEM((1, pair_mu.shape[1]), jnp.int32),
            pltpu.SMEM((1, lists), jnp.int32),
            pltpu.SMEM((1, pair_mu.shape[1]), jnp.int32),
            pltpu.VMEM((2, 8, 128), jnp.int32),
            pltpu.VMEM((N_ORB, 2, 8, 128), jnp.int32),
            pltpu.VMEM((8, 128), f32),
            pltpu.VMEM((8, 128), f32),
            pltpu.VMEM((2, 3, 8, 128), f32),
            pltpu.VMEM((2, TILE, 128), f32),
            pltpu.VMEM((4, half, TILE, 128), bf16),
            pltpu.VMEM((4, half, TILE, 128), bf16),
            pltpu.VMEM((half, TILE, 128), f32),
            pltpu.VMEM((4, half, TILE, 128), bf16),
            pltpu.VMEM((3, half, TILE, 128), bf16),
            pltpu.VMEM((cap + 2, TILE, 128), bf16),
            pltpu.VMEM((4, 4, TILE, 128), bf16),
            pltpu.VMEM((4, 4, TILE, 128), bf16),
            pltpu.VMEM((3, 4, TILE, 128), bf16),
            pltpu.VMEM((3, 4, TILE, 128), bf16),
            pltpu.VMEM((4, TILE, 128), f32),
            pltpu.VMEM((4, TILE, 128), f32),
            pltpu.VMEM((3, TILE, 128), f32),
            pltpu.VMEM((3, TILE, 128), f32),
            dma((QS,)),
            dma((QS, N_ORB - 1)),
            dma((QS, N_ORB)),
            dma((N_ORB - 1,)),
            dma((N_ORB,)),
            dma((4,)),
            dma((4,)),
            dma(()),
            dma(()),
            dma((2, 3)),
            dma((2, 3)),
            dma((5, 3)),
            dma((5, 3)),
        ],
        compiler_params=pltpu.CompilerParams(
            collective_id=identity, has_side_effects=True, vmem_limit_bytes=LIMIT
        ),
        name="exchange",
    )(mu, nu, live, support, coeffs, pair_mu, pair_nu, ints)


def on_device(integrals, tile_mu, tile_nu, live_count, support, coeffs, pair_mu, pair_nu):
    args = (tile_mu, tile_nu, live_count, support.T, coeffs, pair_mu[None, :], pair_nu[None, :], integrals)

    out, over = exchange(POOL, CAP, 0, *args)
    return lax.cond(over[0] == 0, lambda: out, lambda: exchange(2 * OCC, NPAIR // N_ORB, 1, *args)[0])


def solution(mesh):
    return jax.shard_map(
        on_device,
        mesh=mesh,
        in_specs=(
            P(("aux", "orb"), None, None),
            P(("aux", "orb")),
            P(("aux", "orb")),
            P(("aux", "orb")),
            P(),
            P(),
            P(),
            P(),
        ),
        out_specs=P(("aux", "orb"), None),
        check_vma=False,
    )
```

```python
import functools

import jax
import jax.numpy as jnp
from jax import lax
from jax.experimental import pallas as pl
from jax.experimental.pallas import tpu as pltpu
from jax.sharding import PartitionSpec as P

TILE = 64
AUX_DEV = 256
OCC = 64
SUP = 16
WT = 32
N_ORB = 8
POOL = 88
NPAIR = 512
SLOTS = 16
QS = 4
COLS = AUX_DEV * TILE // (QS * N_ORB)
ROWS = COLS // 128 * OCC
HALF = TILE // 2
CAP = 20
MESH = pl.DeviceIdType.MESH
VMEM = pl.BlockSpec(memory_space=pltpu.VMEM)
SMEM = pl.BlockSpec(memory_space=pltpu.SMEM)
LIMIT = 60 * 1024 * 1024

OFFSETS = ((2, 0), (2, 1), (1, 0), (3, 0), (1, 1), (3, 1), (0, 1))


STEPS = (2, 1, 3)


def chunk_rows(pool):
    top = pool // 16 * 16
    return top, COLS // 128 * top, COLS // 128 * top + (COLS // 256 * 16 if pool > top else 0)


def exchange_kernel(
    pool,
    cap,
    mu_ref,
    nu_ref,
    live_ref,
    support_hbm,
    coeffs_hbm,
    pm_hbm,
    pn_hbm,
    ints_hbm,
    out_ref,
    any_ref,
    support_ref,
    coeffs_ref,
    pm_ref,
    pn_ref,
    ints,
    sbuf,
    rbuf,
    xbuf,
    tiles,
    unpack,
    merge,
    stack,
    first,
    acc,
    order,
    index,
    order_smem,
    index_smem,
    mine,
    mus,
    over,
    row,
    overs,
    done,
    gsend,
    gpeer,
    kept_tiles,
    sz,
    rz,
    blocks,
    e_a,
    e_b,
    r1_a,
    r1_b,
    s2_a,
    s2_b,
    r2_a,
    r2_b,
    small_sem,
    in_sem,
    send_sem,
    recv_sem,
    mu_send,
    mu_recv,
    g_send,
    g_recv,
    order_sem,
    index_sem,
    tell_send,
    tell_recv,
    ring_send,
    ring_recv,
):
    top, tops, _ = chunk_rows(pool)
    ragged = pool > top
    lists = order.shape[1]
    aux = lax.axis_index("aux")
    me = lax.axis_index("orb")
    y, x = aux // 4, lax.rem(aux, 4)
    z, core = me // 2, lax.rem(me, 2)
    others = [lax.rem(z + dz, 4) * 2 + lax.rem(core + dc, 2) for dz, dc in OFFSETS]
    peer = others[-1]
    place = {"x": x, "y": y, "z": z}

    def along(axis, step):
        if axis == "x":
            return (y * 4 + lax.rem(x + step, 4), me)
        if axis == "y":
            return (lax.rem(y + step, 4) * 4 + x, me)
        return (aux, lax.rem(z + step, 4) * 2 + core)

    def load(q):
        return pltpu.make_async_copy(
            ints_hbm.at[:, :, pl.ds(pl.multiple_of(q * COLS * N_ORB, COLS * N_ORB), COLS * N_ORB)],
            ints.at[q],
            in_sem.at[q],
        )

    barrier = pltpu.get_barrier_semaphore()
    for other in others:
        pl.semaphore_signal(barrier, inc=1, device_id=(aux, other), device_id_type=MESH)
    for axis in "xy":
        for step in STEPS:
            pl.semaphore_signal(barrier, inc=1, device_id=along(axis, step), device_id_type=MESH)
    small = [
        pltpu.make_async_copy(source, target, small_sem.at[i])
        for i, (source, target) in enumerate(
            ((support_hbm, support_ref), (coeffs_hbm, coeffs_ref), (pm_hbm, pm_ref), (pn_hbm, pn_ref))
        )
    ]
    for copy in small:
        copy.start()
    for q in range(QS):
        load(q).start()

    lane = lax.broadcasted_iota(jnp.int32, (OCC, 128), 1)
    low = lane < TILE
    one = (
        lax.broadcasted_iota(jnp.int32, (SUP, SUP), 0) == lax.broadcasted_iota(jnp.int32, (SUP, SUP), 1)
    ).astype(jnp.float32)
    small[0].wait()
    support = lax.dot_general(
        support_ref[...].astype(jnp.float32), one, (((0,), (0,)), ((), ())), preferred_element_type=jnp.float32
    )
    for j in range(SUP):
        tiles[j] = jnp.broadcast_to(support[:, j : j + 1], (OCC, 128))
    small[1].wait()
    halves = []
    for s in range(2):
        total = jnp.zeros((OCC, 128), jnp.float32)
        nu = nu_ref[s].astype(jnp.float32)
        for jj in range(SUP // 2):
            tile = jnp.where(low, tiles[2 * jj], tiles[2 * jj + 1])
            block = coeffs_ref[:, jj * 128 : (jj + 1) * 128].astype(jnp.float32)
            total = total + jnp.where(tile == nu, block, 0.0)
        total = total + pltpu.roll(total, 64, 1)
        live = jnp.where(s < live_ref[0], 1.0, 0.0)
        keep = low if s == 0 else jnp.logical_not(low)
        halves.append(jnp.where(keep, total * live, 0.0))
    coef = jnp.concatenate(halves, axis=0).astype(jnp.bfloat16)

    slot = lax.rem(lax.broadcasted_iota(jnp.int32, (8, 128), 0), 2)
    mine[0] = jnp.where(slot < live_ref[0], jnp.where(slot == 0, mu_ref[0], mu_ref[1]), -1)
    mine[1] = jnp.where(slot < live_ref[0], jnp.where(slot == 0, nu_ref[0], nu_ref[1]), -1)

    square = (2 * OCC, 2 * OCC)
    to, at = lax.broadcasted_iota(jnp.int32, square, 0), lax.broadcasted_iota(jnp.int32, square, 1)
    before = jnp.where(at < to, 1.0, 0.0).astype(jnp.bfloat16)

    def placement(nus):
        used = []
        for s in range(2):
            nu = nus[s : s + 1].astype(jnp.float32)
            count = jnp.zeros((OCC, 128), jnp.float32)
            for j in range(SUP):
                count = count + jnp.where(tiles[j] == nu, 1.0, 0.0)
            used.append(count)
        used = jnp.concatenate(used, axis=0)
        rank = jnp.dot(before, used.astype(jnp.bfloat16), preferred_element_type=jnp.float32)
        last = slice(2 * OCC - 1, 2 * OCC)
        placed = jnp.where(rank == at.astype(jnp.float32), used, 0.0)
        return placed.astype(jnp.bfloat16), rank[last] + used[last]

    own, _ = placement(mine[1])
    packed = lax.dot_general(own, coef, (((0,), (0,)), ((), ())), preferred_element_type=jnp.float32)
    packed = packed[:pool].astype(jnp.bfloat16)

    def mu_copy(t, device):
        return pltpu.make_async_remote_copy(
            src_ref=mine,
            dst_ref=mus.at[device],
            send_sem=mu_send.at[t],
            recv_sem=mu_recv.at[device],
            device_id=(aux, others[t]),
            device_id_type=MESH,
        )

    def data_copy(q, t, device):
        return pltpu.make_async_remote_copy(
            src_ref=sbuf.at[q, t],
            dst_ref=rbuf.at[q, device],
            send_sem=send_sem.at[q, t],
            recv_sem=recv_sem.at[q, device],
            device_id=(aux, others[t]),
            device_id_type=MESH,
        )

    def swap(part, step):
        zz = lax.rem(z + step, 4)
        return pltpu.make_async_remote_copy(
            src_ref=gsend.at[part, zz],
            dst_ref=gpeer.at[part, zz],
            send_sem=g_send.at[part, step],
            recv_sem=g_recv.at[part, step],
            device_id=(aux, peer),
            device_id_type=MESH,
        )

    def products(q, dest, store):
        block = ints[q, :, :, pl.ds(pl.multiple_of(dest * COLS, COLS), COLS)].reshape(2 * TILE, COLS)
        res = jnp.dot(packed, block, preferred_element_type=jnp.float32)
        for p in range(COLS // 128):
            store(p * top, res[:top, p * 128 : (p + 1) * 128].astype(jnp.bfloat16))
        if ragged:
            for p in range(0, COLS // 128, 2):
                last = [res[top:, (p + i) * 128 : (p + i + 1) * 128] for i in range(2)]
                store(tops + p * 8, jnp.concatenate(last, axis=0).astype(jnp.bfloat16))

    def tell(stage, axis, source):
        return [
            pltpu.make_async_remote_copy(
                src_ref=source,
                dst_ref=overs.at[stage, 3 - step],
                send_sem=tell_send.at[stage, step - 1],
                recv_sem=tell_recv.at[stage, 3 - step],
                device_id=along(axis, step),
                device_id_type=MESH,
            )
            for step in STEPS
        ]

    pl.semaphore_wait(barrier, len(others) + 6)
    for t in range(len(others)):
        mu_copy(t, me).start()

    @pl.loop(0, QS)
    def _(q):
        load(q).wait()
        for t, other in enumerate(others):

            def to_send(row, value):
                sbuf[q, t, row : row + value.shape[0], :] = value

            products(q, other, to_send)
            data_copy(q, t, me).start()

        def to_own(row, value):
            rbuf[q, me, row : row + value.shape[0], :] = value

        products(q, me, to_own)

    mus[me] = mine[...]
    for t, other in enumerate(others):
        mu_copy(t, other).wait_recv()
    over[...] = jnp.zeros_like(over)

    @pl.loop(0, N_ORB)
    def _(source):
        placed, rows = placement(mus[source, 1])
        unpack[source] = placed.astype(jnp.float32).T
        over[...] = jnp.maximum(over[...], jnp.where(rows > pool, 1.0, 0.0))

    def mu_of(slot):
        return mus[slot // 2, 0, slot % 2 : slot % 2 + 1]

    for s in range(SLOTS):
        is_first = jnp.ones((1, 128), jnp.int32)
        for t in range(s):
            is_first = jnp.where(mu_of(t) == mu_of(s), 0, is_first)
        first[s : s + 1] = jnp.where(mu_of(s) >= 0, is_first, 0)
    low_row = low[:1]
    if ragged:
        stack[N_ORB * top :] = jnp.zeros((N_ORB * 16, 128), jnp.float32)
    for pair in range(N_ORB):

        @pl.loop(0, N_ORB)
        def _(source):
            def shares(slot, s):
                same = mus[source, 0, s : s + 1] == mu_of(slot)
                return jnp.where(same, first[slot : slot + 1], 0).astype(jnp.float32)

            kept = jnp.where(low_row, shares(2 * pair, 0), shares(2 * pair + 1, 1))
            turned = jnp.where(low_row, shares(2 * pair, 1), shares(2 * pair + 1, 0))
            placed = unpack[source]
            both = placed * kept + pltpu.roll(placed, 64, 1) * turned
            stack[pl.ds(pl.multiple_of(source * top, top), top)] = both[:top]
            if ragged:
                stack[pl.ds(pl.multiple_of(N_ORB * top + source * 16, 16), 8)] = both[top:pool]

        merged = stack[...].T
        at = slice(pair % 4 * 128, (pair % 4 + 1) * 128)
        merge[0, pair // 4, at] = merged.astype(jnp.bfloat16)
        if ragged:
            turned = pltpu.roll(merged[:, N_ORB * top :], 8, 1)
            merged = jnp.concatenate([merged[:, : N_ORB * top], turned], axis=1)
            merge[1, pair // 4, at] = merged.astype(jnp.bfloat16)

    for copy in small[2:]:
        copy.wait()
    k = lax.broadcasted_iota(jnp.int32, pm_ref.shape, 1)
    u = jnp.full(pm_ref.shape, -1, jnp.int32)
    v = jnp.full(pm_ref.shape, -1, jnp.int32)
    for s in range(SLOTS):
        known = first[s : s + 1, :1] > 0
        tile = mu_of(s)[:, :1]
        u = jnp.where(jnp.logical_and(known, pm_ref[...] == tile), s, u)
        v = jnp.where(jnp.logical_and(known, pn_ref[...] == tile), s, v)
    active = jnp.logical_and(u >= 0, v >= 0)
    npair = pm_ref.shape[1]
    square = (npair, npair)
    to, at = lax.broadcasted_iota(jnp.int32, square, 0), lax.broadcasted_iota(jnp.int32, square, 1)
    ahead = jnp.where(jnp.logical_and(to < at, ((to ^ at) & 28) == 0), 1.0, 0.0).astype(jnp.bfloat16)
    flags = jnp.broadcast_to(jnp.where(active, 1.0, 0.0), (8, npair)).astype(jnp.bfloat16)
    rank = jnp.dot(flags, ahead, preferred_element_type=jnp.float32)[:1].astype(jnp.int32)
    spill = jnp.logical_and(active, rank >= cap)
    over[...] = jnp.maximum(over[...], jnp.max(jnp.where(spill, 1.0, 0.0)))
    listed = jnp.logical_and(active, rank < cap)
    at_list = jnp.where(listed, ((k >> 2) & 7) * cap + rank, -1)
    chosen = jnp.where(lax.broadcasted_iota(jnp.int32, (lists, npair), 0) == at_list, 1.0, 0.0)
    tiles_of = jnp.broadcast_to((u * SLOTS + v).astype(jnp.float32), (8, npair)).astype(jnp.bfloat16)
    order[...] = lax.dot_general(
        tiles_of, chosen.astype(jnp.bfloat16), (((1,), (1,)), ((), ())), preferred_element_type=jnp.float32
    )[:1].astype(jnp.int32)
    index[...] = jnp.where(listed, ((rank + k) & 1) * (cap // 2 + 1) + (rank >> 1), cap // 2)
    to_smem = [
        pltpu.make_async_copy(order, order_smem, order_sem),
        pltpu.make_async_copy(index, index_smem, index_sem),
    ]
    for copy in to_smem:
        copy.start()
    for part in range(2):
        blocks[part, cap // 2] = jnp.zeros((HALF, 128), jnp.bfloat16)

    tell_x = tell(0, "x", over)
    for copy in tell_x:
        copy.start()
    for copy in tell_x:
        copy.wait_recv()
    row[...] = over[...] + overs[0, 0] + overs[0, 1] + overs[0, 2]
    tell_y = tell(1, "y", row)
    for copy in tell_y:
        copy.start()

    acc[...] = jnp.zeros_like(acc)

    def spread(q):
        def column(p):
            parts = [rbuf[q, source, p * top : (p + 1) * top] for source in range(N_ORB)]
            if ragged:
                at = tops + p // 2 * 16
                parts += [rbuf[q, source, at : at + 16] for source in range(N_ORB)]
            return jnp.concatenate(parts, axis=0)

        for odd_p in range(2):
            data = jnp.concatenate([column(p) for p in range(odd_p, COLS // 128, 2)], axis=1)
            for half in range(2):
                res = jnp.dot(merge[odd_p if ragged else 0, half], data, preferred_element_type=jnp.float32)
                for n, p in enumerate(range(odd_p, COLS // 128, 2)):
                    lanes = slice(n * 128, (n + 1) * 128)
                    for i in range(4):
                        a = res[i * 128 : i * 128 + OCC, lanes]
                        b = res[i * 128 + OCC : (i + 1) * 128, lanes]
                        even = jnp.where(low, a, pltpu.roll(b, 64, 1))
                        odd = jnp.where(low, pltpu.roll(a, 64, 1), b)
                        xbuf[half * 4 + i, p * OCC : (p + 1) * OCC] = even.astype(jnp.bfloat16)
                        xbuf[half * 4 + i, ROWS + p * OCC : ROWS + (p + 1) * OCC] = odd.astype(jnp.bfloat16)

    def gram(r):
        left = jnp.concatenate([xbuf[2 * r], xbuf[2 * r + 1]], axis=1)
        for c in range(4):
            right = jnp.concatenate([xbuf[2 * c], xbuf[2 * c + 1]], axis=1)
            res = lax.dot_general(
                left, right, (((0,), (0,)), ((), ())), preferred_element_type=jnp.float32
            )
            for i in range(4):
                for h in range(2):
                    acc[(r * 4 + i) * 8 + c * 2 + h] += res[i * TILE : (i + 1) * TILE, h * 128 : (h + 1) * 128]

    @pl.loop(0, QS)
    def _(q):
        for t, other in enumerate(others):
            data_copy(q, t, other).wait_recv()
        spread(q)

        @pl.loop(0, 4)
        def _(r):
            gram(r)

    for copy in to_smem:
        copy.wait()

    def ring(part, stage, axis, source, landing, step):
        at = part * 5 + stage
        copy = pltpu.make_async_remote_copy(
            src_ref=source.at[part, lax.rem(place[axis] + step, 4)],
            dst_ref=landing.at[part, 3 - step],
            send_sem=ring_send.at[at, step - 1],
            recv_sem=ring_recv.at[at, 3 - step],
            device_id=along(axis, step),
            device_id_type=MESH,
        )
        copy.start()
        return copy

    low = low[:HALF]

    def packed_tiles(part, owner, b):
        at = owner * cap + 2 * b
        t0, t1 = order_smem[0, at] & 255, order_smem[0, at + 1] & 255
        rows = slice(part * HALF, (part + 1) * HALF)
        tile0, tile1 = acc[t0 >> 1, rows], acc[t1 >> 1, rows]
        in_place = jnp.broadcast_to(jnp.where(low_row, t0 & 1, 1 - (t1 & 1)), low.shape) == 0
        straight, crossed = jnp.where(low, tile0, tile1), jnp.where(low, tile1, tile0)
        return jnp.where(in_place, straight, pltpu.roll(crossed, 64, 1))

    unroll = 10 if cap % 10 == 0 else 4

    def give(part, step):
        zz = lax.rem(z + step, 4)

        @pl.loop(0, cap // 2, unroll=unroll)
        def _(b):
            gsend[part, zz, b] = packed_tiles(part, zz * 2 + 1 - core, b).astype(jnp.bfloat16)

        swap(part, step).start()

    z_copies = ([], [])

    def take(part, step):
        zz = lax.rem(z + step, 4)

        @pl.loop(0, cap // 2, unroll=unroll)
        def _(b):
            kept_tiles[b] = packed_tiles(part, zz * 2 + core, b)

        swap(part, step).wait_recv()
        sz[part, zz] = (kept_tiles[...] + gpeer[part, zz].astype(jnp.float32)).astype(jnp.bfloat16)
        if step:
            z_copies[part].append(ring(part, 0, "z", sz, rz, step))

    turns = STEPS + (0,)
    todo = [(part, step) for part in range(2) for step in turns]
    give(*todo[0])
    for i in range(8):
        if i < 7:
            give(*todo[i + 1])
        take(*todo[i])

    def block(part, yy, xx, j):
        k = (yy * 4 + xx) * 32 + z * 8 + core * 4 + 2 * j
        left, right = (jnp.clip(index_smem[0, k + h], 0, cap + 1) for h in range(2))
        return jnp.where(low, blocks[part, left], blocks[part, right])

    one_a, one_b, two_a, two_b = ([], []), ([], []), ([], []), ([], [])
    for part in range(2):
        for copy in z_copies[part]:
            copy.wait_recv()
        for b in range(cap // 2):
            total = sz[part, z, b].astype(jnp.float32)
            for n in range(3):
                total = total + rz[part, n, b].astype(jnp.float32)
            blocks[part, b] = total.astype(jnp.bfloat16)
            blocks[part, cap // 2 + 1 + b] = pltpu.roll(total, 64, 1).astype(jnp.bfloat16)
        for step in turns:
            xx, yy = lax.rem(x + step, 4), lax.rem(y + step, 4)
            for i in range(4):
                e_a[part, xx, i] = block(part, i, xx, 0)
            if step:
                one_a[part].append(ring(part, 1, "x", e_a, r1_a, step))
            for i in range(4):
                e_b[part, yy, i] = block(part, yy, i, 1)
            if step:
                one_b[part].append(ring(part, 2, "y", e_b, r1_b, step))

    for part in range(2):
        for stage, copies, more, axis, then, e, r1, s2, r2 in (
            (3, one_a, two_a, "x", "y", e_a, r1_a, s2_a, r2_a),
            (4, one_b, two_b, "y", "x", e_b, r1_b, s2_b, r2_b),
        ):
            for copy in copies[part]:
                copy.wait_recv()
            for step in turns:
                i = lax.rem(place[then] + step, 4)
                total = e[part, place[axis], i].astype(jnp.float32)
                for n in range(3):
                    total = total + r1[part, n, i].astype(jnp.float32)
                s2[part, i] = total
                if step:
                    more[part].append(ring(part, stage, then, s2, r2, step))

    for copy in tell_y:
        copy.wait_recv()
    found = jnp.max(row[...] + overs[1, 0] + overs[1, 1] + overs[1, 2])
    any_ref[0] = jnp.where(found > 0.5, 1, 0)

    for part in range(2):
        rows = slice(part * HALF, (part + 1) * HALF)
        for j, copies, then, s2, r2 in ((0, two_a, "y", s2_a, r2_a), (1, two_b, "x", s2_b, r2_b)):
            for copy in copies[part]:
                copy.wait_recv()
            done[j, rows] = s2[part, place[then]] + r2[part, 0] + r2[part, 1] + r2[part, 2]
    low = lax.broadcasted_iota(jnp.int32, (TILE // 2, 128), 1) < TILE
    for i in range(2):
        even = done[i, pl.ds(0, TILE // 2, stride=2), :]
        odd = done[i, pl.ds(1, TILE // 2, stride=2), :]
        left = jnp.where(low, even, pltpu.roll(odd, 64, 1))
        right = jnp.where(low, pltpu.roll(even, 64, 1), odd)
        for m in range(TILE // 2):
            out_ref[2 * i : 2 * i + 1, m * 128 : (m + 1) * 128] = left[m : m + 1]
            out_ref[2 * i + 1 : 2 * i + 2, m * 128 : (m + 1) * 128] = right[m : m + 1]

    for copies in (*z_copies, *one_a, *one_b, *two_a, *two_b, tell_x, tell_y):
        for copy in copies:
            copy.wait_send()
    for part in range(2):
        for step in range(4):
            swap(part, step).wait_send()
    for t in range(len(others)):
        mu_copy(t, me).wait_send()

    @pl.loop(0, QS)
    def _(q):
        for t in range(len(others)):
            data_copy(q, t, me).wait_send()


def exchange(pool, cap, identity, mu, nu, live, support, coeffs, pair_mu, pair_nu, ints):
    top, _, rows = chunk_rows(pool)
    depth = N_ORB * (top + (16 if pool > top else 0))
    dma = pltpu.SemaphoreType.DMA
    bf16, f32 = jnp.bfloat16, jnp.float32
    half = cap // 2
    lists = pl.cdiv(N_ORB * cap, 128) * 128

    return pl.pallas_call(
        functools.partial(exchange_kernel, pool, cap),
        out_shape=(
            jax.ShapeDtypeStruct((4, TILE * TILE), f32),
            jax.ShapeDtypeStruct((1,), jnp.int32),
        ),
        in_specs=[SMEM] * 3 + [pl.BlockSpec(memory_space=pl.ANY)] * 5,
        out_specs=(VMEM, SMEM),
        scratch_shapes=[
            *(pltpu.VMEM(array.shape, array.dtype) for array in (support, coeffs, pair_mu, pair_nu)),
            pltpu.VMEM((QS, 2, TILE, COLS * N_ORB), bf16),
            pltpu.VMEM((QS, N_ORB - 1, rows, 128), bf16),
            pltpu.VMEM((QS, N_ORB, rows, 128), bf16),
            pltpu.VMEM((N_ORB, 2 * ROWS, 128), bf16),
            pltpu.VMEM((SUP, OCC, 128), f32),
            pltpu.VMEM((N_ORB, 2 * OCC, 2 * OCC), f32),
            pltpu.VMEM((2 if pool > top else 1, 2, 8 * OCC, depth), bf16),
            pltpu.VMEM((depth, 128), f32),
            pltpu.VMEM((SLOTS, 128), jnp.int32),
            pltpu.VMEM((SLOTS * SLOTS // 2, TILE, 128), f32),
            pltpu.VMEM((1, lists), jnp.int32),
            pltpu.VMEM((1, pair_mu.shape[1]), jnp.int32),
            pltpu.SMEM((1, lists), jnp.int32),
            pltpu.SMEM((1, pair_mu.shape[1]), jnp.int32),
            pltpu.VMEM((2, 8, 128), jnp.int32),
            pltpu.VMEM((N_ORB, 2, 8, 128), jnp.int32),
            pltpu.VMEM((8, 128), f32),
            pltpu.VMEM((8, 128), f32),
            pltpu.VMEM((2, 3, 8, 128), f32),
            pltpu.VMEM((2, TILE, 128), f32),
            pltpu.VMEM((2, 4, half, HALF, 128), bf16),
            pltpu.VMEM((2, 4, half, HALF, 128), bf16),
            pltpu.VMEM((half, HALF, 128), f32),
            pltpu.VMEM((2, 4, half, HALF, 128), bf16),
            pltpu.VMEM((2, 3, half, HALF, 128), bf16),
            pltpu.VMEM((2, cap + 2, HALF, 128), bf16),
            pltpu.VMEM((2, 4, 4, HALF, 128), bf16),
            pltpu.VMEM((2, 4, 4, HALF, 128), bf16),
            pltpu.VMEM((2, 3, 4, HALF, 128), bf16),
            pltpu.VMEM((2, 3, 4, HALF, 128), bf16),
            pltpu.VMEM((2, 4, HALF, 128), f32),
            pltpu.VMEM((2, 4, HALF, 128), f32),
            pltpu.VMEM((2, 3, HALF, 128), f32),
            pltpu.VMEM((2, 3, HALF, 128), f32),
            dma((4,)),
            dma((QS,)),
            dma((QS, N_ORB - 1)),
            dma((QS, N_ORB)),
            dma((N_ORB - 1,)),
            dma((N_ORB,)),
            dma((2, 4)),
            dma((2, 4)),
            dma(()),
            dma(()),
            dma((2, 3)),
            dma((2, 3)),
            dma((10, 3)),
            dma((10, 3)),
        ],
        compiler_params=pltpu.CompilerParams(
            collective_id=identity, has_side_effects=True, vmem_limit_bytes=LIMIT
        ),
        name="exchange",
    )(mu, nu, live, support, coeffs, pair_mu, pair_nu, ints)


def on_device(integrals, tile_mu, tile_nu, live_count, support, coeffs, pair_mu, pair_nu):
    args = (tile_mu, tile_nu, live_count, support.T, coeffs, pair_mu[None, :], pair_nu[None, :], integrals)

    out, over = exchange(POOL, CAP, 0, *args)
    return lax.cond(over[0] == 0, lambda: out, lambda: exchange(2 * OCC, NPAIR // N_ORB, 1, *args)[0])


def solution(mesh):
    return jax.shard_map(
        on_device,
        mesh=mesh,
        in_specs=(
            P(("aux", "orb"), None, None),
            P(("aux", "orb")),
            P(("aux", "orb")),
            P(("aux", "orb")),
            P(),
            P(),
            P(),
            P(),
        ),
        out_specs=P(("aux", "orb"), None),
        check_vma=False,
    )
```

```python
import functools

import jax
import jax.numpy as jnp
from jax import lax
from jax.experimental import pallas as pl
from jax.experimental.pallas import tpu as pltpu
from jax.sharding import PartitionSpec as P

TILE = 64
AUX_DEV = 256
OCC = 64
SUP = 16
WT = 32
N_ORB = 8
POOL = 88
NPAIR = 512
SLOTS = 16
QS = 4
COLS = AUX_DEV * TILE // (QS * N_ORB)
ROWS = COLS // 128 * OCC
HALF = TILE // 2
CAP = 20
MESH = pl.DeviceIdType.MESH
VMEM = pl.BlockSpec(memory_space=pltpu.VMEM)
SMEM = pl.BlockSpec(memory_space=pltpu.SMEM)
LIMIT = 60 * 1024 * 1024

OFFSETS = ((2, 0), (2, 1), (1, 0), (3, 0), (1, 1), (3, 1), (0, 1))


STEPS = (2, 1, 3)


def chunk_rows(pool):
    top = pool // 16 * 16
    return top, COLS // 128 * top, COLS // 128 * top + (COLS // 256 * 16 if pool > top else 0)


def exchange_kernel(
    pool,
    cap,
    mu_ref,
    nu_ref,
    live_hbm,
    support_hbm,
    coeffs_hbm,
    pm_hbm,
    pn_hbm,
    ints_hbm,
    out_ref,
    any_ref,
    live_ref,
    support_ref,
    coeffs_ref,
    pm_ref,
    pn_ref,
    ints,
    sbuf,
    rbuf,
    xbuf,
    tiles,
    unpack,
    merge,
    stack,
    first,
    acc,
    order,
    index,
    order_smem,
    index_smem,
    mine,
    mus,
    over,
    row,
    overs,
    done,
    gsend,
    gpeer,
    kept_tiles,
    sz,
    rz,
    blocks,
    e_a,
    e_b,
    r1_a,
    r1_b,
    s2_a,
    s2_b,
    r2_a,
    r2_b,
    small_sem,
    in_sem,
    send_sem,
    recv_sem,
    mu_send,
    mu_recv,
    g_send,
    g_recv,
    order_sem,
    index_sem,
    tell_send,
    tell_recv,
    ring_send,
    ring_recv,
):
    top, tops, _ = chunk_rows(pool)
    ragged = pool > top
    lists = order.shape[1]
    aux = lax.axis_index("aux")
    me = lax.axis_index("orb")
    y, x = aux // 4, lax.rem(aux, 4)
    z, core = me // 2, lax.rem(me, 2)
    others = [lax.rem(z + dz, 4) * 2 + lax.rem(core + dc, 2) for dz, dc in OFFSETS]
    peer = others[-1]
    place = {"x": x, "y": y, "z": z}

    def along(axis, step):
        if axis == "x":
            return (y * 4 + lax.rem(x + step, 4), me)
        if axis == "y":
            return (lax.rem(y + step, 4) * 4 + x, me)
        return (aux, lax.rem(z + step, 4) * 2 + core)

    def load(q):
        return pltpu.make_async_copy(
            ints_hbm.at[:, :, pl.ds(pl.multiple_of(q * COLS * N_ORB, COLS * N_ORB), COLS * N_ORB)],
            ints.at[q],
            in_sem.at[q],
        )

    barrier = pltpu.get_barrier_semaphore()
    for other in others:
        pl.semaphore_signal(barrier, inc=1, device_id=(aux, other), device_id_type=MESH)
    for axis in "xy":
        for step in STEPS:
            pl.semaphore_signal(barrier, inc=1, device_id=along(axis, step), device_id_type=MESH)
    small = [
        pltpu.make_async_copy(source, target, small_sem.at[i])
        for i, (source, target) in enumerate(
            (
                (support_hbm, support_ref),
                (coeffs_hbm, coeffs_ref),
                (live_hbm, live_ref),
                (pm_hbm, pm_ref),
                (pn_hbm, pn_ref),
            )
        )
    ]
    for copy in small:
        copy.start()
    for q in range(QS):
        load(q).start()

    lane = lax.broadcasted_iota(jnp.int32, (OCC, 128), 1)
    low = lane < TILE
    one = (
        lax.broadcasted_iota(jnp.int32, (SUP, SUP), 0) == lax.broadcasted_iota(jnp.int32, (SUP, SUP), 1)
    ).astype(jnp.float32)
    small[0].wait()
    support = lax.dot_general(
        support_ref[...].astype(jnp.float32), one, (((0,), (0,)), ((), ())), preferred_element_type=jnp.float32
    )
    for j in range(SUP):
        tiles[j] = jnp.broadcast_to(support[:, j : j + 1], (OCC, 128))
    small[1].wait()
    small[2].wait()
    halves = []
    for s in range(2):
        total = jnp.zeros((OCC, 128), jnp.float32)
        nu = nu_ref[s].astype(jnp.float32)
        for jj in range(SUP // 2):
            tile = jnp.where(low, tiles[2 * jj], tiles[2 * jj + 1])
            block = coeffs_ref[:, jj * 128 : (jj + 1) * 128].astype(jnp.float32)
            total = total + jnp.where(tile == nu, block, 0.0)
        total = total + pltpu.roll(total, 64, 1)
        live = jnp.where(s < live_ref[0], 1.0, 0.0)
        keep = low if s == 0 else jnp.logical_not(low)
        halves.append(jnp.where(keep, total * live, 0.0))
    coef = jnp.concatenate(halves, axis=0).astype(jnp.bfloat16)

    slot = lax.rem(lax.broadcasted_iota(jnp.int32, (8, 128), 0), 2)
    mine[0] = jnp.where(slot < live_ref[0], jnp.where(slot == 0, mu_ref[0], mu_ref[1]), -1)
    mine[1] = jnp.where(slot < live_ref[0], jnp.where(slot == 0, nu_ref[0], nu_ref[1]), -1)

    square = (2 * OCC, 2 * OCC)
    to, at = lax.broadcasted_iota(jnp.int32, square, 0), lax.broadcasted_iota(jnp.int32, square, 1)
    before = jnp.where(at < to, 1.0, 0.0).astype(jnp.bfloat16)

    def placement(nus):
        used = []
        for s in range(2):
            nu = nus[s : s + 1].astype(jnp.float32)
            count = jnp.zeros((OCC, 128), jnp.float32)
            for j in range(SUP):
                count = count + jnp.where(tiles[j] == nu, 1.0, 0.0)
            used.append(count)
        used = jnp.concatenate(used, axis=0)
        rank = jnp.dot(before, used.astype(jnp.bfloat16), preferred_element_type=jnp.float32)
        last = slice(2 * OCC - 1, 2 * OCC)
        placed = jnp.where(rank == at.astype(jnp.float32), used, 0.0)
        return placed.astype(jnp.bfloat16), rank[last] + used[last]

    own, _ = placement(mine[1])
    packed = lax.dot_general(own, coef, (((0,), (0,)), ((), ())), preferred_element_type=jnp.float32)
    packed = packed[:pool].astype(jnp.bfloat16)

    def mu_copy(t, device):
        return pltpu.make_async_remote_copy(
            src_ref=mine,
            dst_ref=mus.at[device],
            send_sem=mu_send.at[t],
            recv_sem=mu_recv.at[device],
            device_id=(aux, others[t]),
            device_id_type=MESH,
        )

    def data_copy(q, t, device):
        return pltpu.make_async_remote_copy(
            src_ref=sbuf.at[q, t],
            dst_ref=rbuf.at[q, device],
            send_sem=send_sem.at[q, t],
            recv_sem=recv_sem.at[q, device],
            device_id=(aux, others[t]),
            device_id_type=MESH,
        )

    def swap(part, step):
        zz = lax.rem(z + step, 4)
        return pltpu.make_async_remote_copy(
            src_ref=gsend.at[part, zz],
            dst_ref=gpeer.at[part, zz],
            send_sem=g_send.at[part, step],
            recv_sem=g_recv.at[part, step],
            device_id=(aux, peer),
            device_id_type=MESH,
        )

    def products(q, dest, store):
        block = ints[q, :, :, pl.ds(pl.multiple_of(dest * COLS, COLS), COLS)].reshape(2 * TILE, COLS)
        res = jnp.dot(packed, block, preferred_element_type=jnp.float32)
        for p in range(COLS // 128):
            store(p * top, res[:top, p * 128 : (p + 1) * 128].astype(jnp.bfloat16))
        if ragged:
            for p in range(0, COLS // 128, 2):
                last = [res[top:, (p + i) * 128 : (p + i + 1) * 128] for i in range(2)]
                store(tops + p * 8, jnp.concatenate(last, axis=0).astype(jnp.bfloat16))

    def tell(stage, axis, source):
        return [
            pltpu.make_async_remote_copy(
                src_ref=source,
                dst_ref=overs.at[stage, 3 - step],
                send_sem=tell_send.at[stage, step - 1],
                recv_sem=tell_recv.at[stage, 3 - step],
                device_id=along(axis, step),
                device_id_type=MESH,
            )
            for step in STEPS
        ]

    pl.semaphore_wait(barrier, len(others) + 6)
    for t in range(len(others)):
        mu_copy(t, me).start()

    @pl.loop(0, QS)
    def _(q):
        load(q).wait()
        for t, other in enumerate(others):

            def to_send(row, value):
                sbuf[q, t, row : row + value.shape[0], :] = value

            products(q, other, to_send)
            data_copy(q, t, me).start()

        def to_own(row, value):
            rbuf[q, me, row : row + value.shape[0], :] = value

        products(q, me, to_own)

    mus[me] = mine[...]
    for t, other in enumerate(others):
        mu_copy(t, other).wait_recv()
    over[...] = jnp.zeros_like(over)

    @pl.loop(0, N_ORB)
    def _(source):
        placed, rows = placement(mus[source, 1])
        unpack[source] = placed.astype(jnp.float32).T
        over[...] = jnp.maximum(over[...], jnp.where(rows > pool, 1.0, 0.0))

    def mu_of(slot):
        return mus[slot // 2, 0, slot % 2 : slot % 2 + 1]

    for s in range(SLOTS):
        is_first = jnp.ones((1, 128), jnp.int32)
        for t in range(s):
            is_first = jnp.where(mu_of(t) == mu_of(s), 0, is_first)
        first[s : s + 1] = jnp.where(mu_of(s) >= 0, is_first, 0)
    low_row = low[:1]
    if ragged:
        stack[N_ORB * top :] = jnp.zeros((N_ORB * 16, 128), jnp.float32)
    for pair in range(N_ORB):

        @pl.loop(0, N_ORB)
        def _(source):
            def shares(slot, s):
                same = mus[source, 0, s : s + 1] == mu_of(slot)
                return jnp.where(same, first[slot : slot + 1], 0).astype(jnp.float32)

            kept = jnp.where(low_row, shares(2 * pair, 0), shares(2 * pair + 1, 1))
            turned = jnp.where(low_row, shares(2 * pair, 1), shares(2 * pair + 1, 0))
            placed = unpack[source]
            both = placed * kept + pltpu.roll(placed, 64, 1) * turned
            stack[pl.ds(pl.multiple_of(source * top, top), top)] = both[:top]
            if ragged:
                stack[pl.ds(pl.multiple_of(N_ORB * top + source * 16, 16), 8)] = both[top:pool]

        merged = stack[...].T
        at = slice(pair % 4 * 128, (pair % 4 + 1) * 128)
        merge[0, pair // 4, at] = merged.astype(jnp.bfloat16)
        if ragged:
            turned = pltpu.roll(merged[:, N_ORB * top :], 8, 1)
            merged = jnp.concatenate([merged[:, : N_ORB * top], turned], axis=1)
            merge[1, pair // 4, at] = merged.astype(jnp.bfloat16)

    for copy in small[3:]:
        copy.wait()
    k = lax.broadcasted_iota(jnp.int32, pm_ref.shape, 1)
    u = jnp.full(pm_ref.shape, -1, jnp.int32)
    v = jnp.full(pm_ref.shape, -1, jnp.int32)
    for s in range(SLOTS):
        known = first[s : s + 1, :1] > 0
        tile = mu_of(s)[:, :1]
        u = jnp.where(jnp.logical_and(known, pm_ref[...] == tile), s, u)
        v = jnp.where(jnp.logical_and(known, pn_ref[...] == tile), s, v)
    active = jnp.logical_and(u >= 0, v >= 0)
    npair = pm_ref.shape[1]
    square = (npair, npair)
    to, at = lax.broadcasted_iota(jnp.int32, square, 0), lax.broadcasted_iota(jnp.int32, square, 1)
    ahead = jnp.where(jnp.logical_and(to < at, ((to ^ at) & 28) == 0), 1.0, 0.0).astype(jnp.bfloat16)
    flags = jnp.broadcast_to(jnp.where(active, 1.0, 0.0), (8, npair)).astype(jnp.bfloat16)
    rank = jnp.dot(flags, ahead, preferred_element_type=jnp.float32)[:1].astype(jnp.int32)
    spill = jnp.logical_and(active, rank >= cap)
    over[...] = jnp.maximum(over[...], jnp.max(jnp.where(spill, 1.0, 0.0)))
    listed = jnp.logical_and(active, rank < cap)
    at_list = jnp.where(listed, ((k >> 2) & 7) * cap + rank, -1)
    chosen = jnp.where(lax.broadcasted_iota(jnp.int32, (lists, npair), 0) == at_list, 1.0, 0.0)
    tiles_of = jnp.broadcast_to((u * SLOTS + v).astype(jnp.float32), (8, npair)).astype(jnp.bfloat16)
    order[...] = lax.dot_general(
        tiles_of, chosen.astype(jnp.bfloat16), (((1,), (1,)), ((), ())), preferred_element_type=jnp.float32
    )[:1].astype(jnp.int32)
    index[...] = jnp.where(listed, ((rank + k) & 1) * (cap // 2 + 1) + (rank >> 1), cap // 2)
    to_smem = [
        pltpu.make_async_copy(order, order_smem, order_sem),
        pltpu.make_async_copy(index, index_smem, index_sem),
    ]
    for copy in to_smem:
        copy.start()
    for part in range(2):
        blocks[part, cap // 2] = jnp.zeros((HALF, 128), jnp.bfloat16)

    tell_x = tell(0, "x", over)
    for copy in tell_x:
        copy.start()
    for copy in tell_x:
        copy.wait_recv()
    row[...] = over[...] + overs[0, 0] + overs[0, 1] + overs[0, 2]
    tell_y = tell(1, "y", row)
    for copy in tell_y:
        copy.start()

    acc[...] = jnp.zeros_like(acc)

    def spread(q):
        def column(p):
            parts = [rbuf[q, source, p * top : (p + 1) * top] for source in range(N_ORB)]
            if ragged:
                at = tops + p // 2 * 16
                parts += [rbuf[q, source, at : at + 16] for source in range(N_ORB)]
            return jnp.concatenate(parts, axis=0)

        for odd_p in range(2):
            data = jnp.concatenate([column(p) for p in range(odd_p, COLS // 128, 2)], axis=1)
            for half in range(2):
                res = jnp.dot(merge[odd_p if ragged else 0, half], data, preferred_element_type=jnp.float32)
                for n, p in enumerate(range(odd_p, COLS // 128, 2)):
                    lanes = slice(n * 128, (n + 1) * 128)
                    for i in range(4):
                        a = res[i * 128 : i * 128 + OCC, lanes]
                        b = res[i * 128 + OCC : (i + 1) * 128, lanes]
                        even = jnp.where(low, a, pltpu.roll(b, 64, 1))
                        odd = jnp.where(low, pltpu.roll(a, 64, 1), b)
                        xbuf[half * 4 + i, p * OCC : (p + 1) * OCC] = even.astype(jnp.bfloat16)
                        xbuf[half * 4 + i, ROWS + p * OCC : ROWS + (p + 1) * OCC] = odd.astype(jnp.bfloat16)

    def gram(r):
        left = jnp.concatenate([xbuf[2 * r], xbuf[2 * r + 1]], axis=1)
        for c in range(4):
            right = jnp.concatenate([xbuf[2 * c], xbuf[2 * c + 1]], axis=1)
            res = lax.dot_general(
                left, right, (((0,), (0,)), ((), ())), preferred_element_type=jnp.float32
            )
            for i in range(4):
                for h in range(2):
                    acc[(r * 4 + i) * 8 + c * 2 + h] += res[i * TILE : (i + 1) * TILE, h * 128 : (h + 1) * 128]

    @pl.loop(0, QS)
    def _(q):
        for t, other in enumerate(others):
            data_copy(q, t, other).wait_recv()
        spread(q)

        @pl.loop(0, 4)
        def _(r):
            gram(r)

    for copy in to_smem:
        copy.wait()

    def ring(part, stage, axis, source, landing, step):
        at = part * 5 + stage
        copy = pltpu.make_async_remote_copy(
            src_ref=source.at[part, lax.rem(place[axis] + step, 4)],
            dst_ref=landing.at[part, 3 - step],
            send_sem=ring_send.at[at, step - 1],
            recv_sem=ring_recv.at[at, 3 - step],
            device_id=along(axis, step),
            device_id_type=MESH,
        )
        copy.start()
        return copy

    low = low[:HALF]

    def packed_tiles(part, owner, b):
        at = owner * cap + 2 * b
        t0, t1 = order_smem[0, at] & 255, order_smem[0, at + 1] & 255
        rows = slice(part * HALF, (part + 1) * HALF)
        tile0, tile1 = acc[t0 >> 1, rows], acc[t1 >> 1, rows]
        in_place = jnp.broadcast_to(jnp.where(low_row, t0 & 1, 1 - (t1 & 1)), low.shape) == 0
        straight, crossed = jnp.where(low, tile0, tile1), jnp.where(low, tile1, tile0)
        return jnp.where(in_place, straight, pltpu.roll(crossed, 64, 1))

    unroll = 10 if cap % 10 == 0 else 4

    def give(part, step):
        zz = lax.rem(z + step, 4)

        @pl.loop(0, cap // 2, unroll=unroll)
        def _(b):
            gsend[part, zz, b] = packed_tiles(part, zz * 2 + 1 - core, b).astype(jnp.bfloat16)

        swap(part, step).start()

    z_copies = ([], [])

    def take(part, step):
        zz = lax.rem(z + step, 4)

        @pl.loop(0, cap // 2, unroll=unroll)
        def _(b):
            kept_tiles[b] = packed_tiles(part, zz * 2 + core, b)

        swap(part, step).wait_recv()
        sz[part, zz] = (kept_tiles[...] + gpeer[part, zz].astype(jnp.float32)).astype(jnp.bfloat16)
        if step:
            z_copies[part].append(ring(part, 0, "z", sz, rz, step))

    turns = STEPS + (0,)
    todo = [(part, step) for part in range(2) for step in turns]
    give(*todo[0])
    for i in range(8):
        if i < 7:
            give(*todo[i + 1])
        take(*todo[i])

    def block(part, yy, xx, j):
        k = (yy * 4 + xx) * 32 + z * 8 + core * 4 + 2 * j
        left, right = (jnp.clip(index_smem[0, k + h], 0, cap + 1) for h in range(2))
        return jnp.where(low, blocks[part, left], blocks[part, right])

    one_a, one_b, two_a, two_b = ([], []), ([], []), ([], []), ([], [])
    for part in range(2):
        for copy in z_copies[part]:
            copy.wait_recv()
        for b in range(cap // 2):
            total = sz[part, z, b].astype(jnp.float32)
            for n in range(3):
                total = total + rz[part, n, b].astype(jnp.float32)
            blocks[part, b] = total.astype(jnp.bfloat16)
            blocks[part, cap // 2 + 1 + b] = pltpu.roll(total, 64, 1).astype(jnp.bfloat16)
        for step in turns:
            xx, yy = lax.rem(x + step, 4), lax.rem(y + step, 4)
            for i in range(4):
                e_a[part, xx, i] = block(part, i, xx, 0)
            if step:
                one_a[part].append(ring(part, 1, "x", e_a, r1_a, step))
            for i in range(4):
                e_b[part, yy, i] = block(part, yy, i, 1)
            if step:
                one_b[part].append(ring(part, 2, "y", e_b, r1_b, step))

    for part in range(2):
        for stage, copies, more, axis, then, e, r1, s2, r2 in (
            (3, one_a, two_a, "x", "y", e_a, r1_a, s2_a, r2_a),
            (4, one_b, two_b, "y", "x", e_b, r1_b, s2_b, r2_b),
        ):
            for copy in copies[part]:
                copy.wait_recv()
            for step in turns:
                i = lax.rem(place[then] + step, 4)
                total = e[part, place[axis], i].astype(jnp.float32)
                for n in range(3):
                    total = total + r1[part, n, i].astype(jnp.float32)
                s2[part, i] = total
                if step:
                    more[part].append(ring(part, stage, then, s2, r2, step))

    for copy in tell_y:
        copy.wait_recv()
    found = jnp.max(row[...] + overs[1, 0] + overs[1, 1] + overs[1, 2])
    any_ref[0] = jnp.where(found > 0.5, 1, 0)

    for part in range(2):
        rows = slice(part * HALF, (part + 1) * HALF)
        for j, copies, then, s2, r2 in ((0, two_a, "y", s2_a, r2_a), (1, two_b, "x", s2_b, r2_b)):
            for copy in copies[part]:
                copy.wait_recv()
            done[j, rows] = s2[part, place[then]] + r2[part, 0] + r2[part, 1] + r2[part, 2]
    low = lax.broadcasted_iota(jnp.int32, (TILE // 2, 128), 1) < TILE
    for i in range(2):
        even = done[i, pl.ds(0, TILE // 2, stride=2), :]
        odd = done[i, pl.ds(1, TILE // 2, stride=2), :]
        left = jnp.where(low, even, pltpu.roll(odd, 64, 1))
        right = jnp.where(low, pltpu.roll(even, 64, 1), odd)
        for m in range(TILE // 2):
            out_ref[2 * i : 2 * i + 1, m * 128 : (m + 1) * 128] = left[m : m + 1]
            out_ref[2 * i + 1 : 2 * i + 2, m * 128 : (m + 1) * 128] = right[m : m + 1]

    for copies in (*z_copies, *one_a, *one_b, *two_a, *two_b, tell_x, tell_y):
        for copy in copies:
            copy.wait_send()
    for part in range(2):
        for step in range(4):
            swap(part, step).wait_send()
    for t in range(len(others)):
        mu_copy(t, me).wait_send()

    @pl.loop(0, QS)
    def _(q):
        for t in range(len(others)):
            data_copy(q, t, me).wait_send()


def exchange(pool, cap, identity, mu, nu, live, support, coeffs, pair_mu, pair_nu, ints):
    top, _, rows = chunk_rows(pool)
    depth = N_ORB * (top + (16 if pool > top else 0))
    dma = pltpu.SemaphoreType.DMA
    bf16, f32 = jnp.bfloat16, jnp.float32
    half = cap // 2
    lists = pl.cdiv(N_ORB * cap, 128) * 128

    return pl.pallas_call(
        functools.partial(exchange_kernel, pool, cap),
        out_shape=(
            jax.ShapeDtypeStruct((4, TILE * TILE), f32),
            jax.ShapeDtypeStruct((1,), jnp.int32),
        ),
        in_specs=[SMEM] * 2 + [pl.BlockSpec(memory_space=pl.ANY)] * 6,
        out_specs=(VMEM, SMEM),
        scratch_shapes=[
            pltpu.SMEM(live.shape, live.dtype),
            *(pltpu.VMEM(array.shape, array.dtype) for array in (support, coeffs, pair_mu, pair_nu)),
            pltpu.VMEM((QS, 2, TILE, COLS * N_ORB), bf16),
            pltpu.VMEM((QS, N_ORB - 1, rows, 128), bf16),
            pltpu.VMEM((QS, N_ORB, rows, 128), bf16),
            pltpu.VMEM((N_ORB, 2 * ROWS, 128), bf16),
            pltpu.VMEM((SUP, OCC, 128), f32),
            pltpu.VMEM((N_ORB, 2 * OCC, 2 * OCC), f32),
            pltpu.VMEM((2 if pool > top else 1, 2, 8 * OCC, depth), bf16),
            pltpu.VMEM((depth, 128), f32),
            pltpu.VMEM((SLOTS, 128), jnp.int32),
            pltpu.VMEM((SLOTS * SLOTS // 2, TILE, 128), f32),
            pltpu.VMEM((1, lists), jnp.int32),
            pltpu.VMEM((1, pair_mu.shape[1]), jnp.int32),
            pltpu.SMEM((1, lists), jnp.int32),
            pltpu.SMEM((1, pair_mu.shape[1]), jnp.int32),
            pltpu.VMEM((2, 8, 128), jnp.int32),
            pltpu.VMEM((N_ORB, 2, 8, 128), jnp.int32),
            pltpu.VMEM((8, 128), f32),
            pltpu.VMEM((8, 128), f32),
            pltpu.VMEM((2, 3, 8, 128), f32),
            pltpu.VMEM((2, TILE, 128), f32),
            pltpu.VMEM((2, 4, half, HALF, 128), bf16),
            pltpu.VMEM((2, 4, half, HALF, 128), bf16),
            pltpu.VMEM((half, HALF, 128), f32),
            pltpu.VMEM((2, 4, half, HALF, 128), bf16),
            pltpu.VMEM((2, 3, half, HALF, 128), bf16),
            pltpu.VMEM((2, cap + 2, HALF, 128), bf16),
            pltpu.VMEM((2, 4, 4, HALF, 128), bf16),
            pltpu.VMEM((2, 4, 4, HALF, 128), bf16),
            pltpu.VMEM((2, 3, 4, HALF, 128), bf16),
            pltpu.VMEM((2, 3, 4, HALF, 128), bf16),
            pltpu.VMEM((2, 4, HALF, 128), f32),
            pltpu.VMEM((2, 4, HALF, 128), f32),
            pltpu.VMEM((2, 3, HALF, 128), f32),
            pltpu.VMEM((2, 3, HALF, 128), f32),
            dma((5,)),
            dma((QS,)),
            dma((QS, N_ORB - 1)),
            dma((QS, N_ORB)),
            dma((N_ORB - 1,)),
            dma((N_ORB,)),
            dma((2, 4)),
            dma((2, 4)),
            dma(()),
            dma(()),
            dma((2, 3)),
            dma((2, 3)),
            dma((10, 3)),
            dma((10, 3)),
        ],
        compiler_params=pltpu.CompilerParams(
            collective_id=identity, has_side_effects=True, vmem_limit_bytes=LIMIT
        ),
        name="exchange",
    )(mu, nu, live, support, coeffs, pair_mu, pair_nu, ints)


def on_device(integrals, tile_mu, tile_nu, live_count, support, coeffs, pair_mu, pair_nu):
    args = (tile_mu, tile_nu, live_count, support.T, coeffs, pair_mu[None, :], pair_nu[None, :], integrals)

    out, over = exchange(POOL, CAP, 0, *args)
    return lax.switch(over[0], (lambda: out, lambda: exchange(2 * OCC, NPAIR // N_ORB, 1, *args)[0]))


def solution(mesh):
    return jax.shard_map(
        on_device,
        mesh=mesh,
        in_specs=(
            P(("aux", "orb"), None, None),
            P(("aux", "orb")),
            P(("aux", "orb")),
            P(("aux", "orb")),
            P(),
            P(),
            P(),
            P(),
        ),
        out_specs=P(("aux", "orb"), None),
        check_vma=False,
    )
```
